32 devices in a mesh: col: 4 (over x, core), depth: 8 (over z, y).
Axes of the slice: x: 2, y: 2, z: 4, core: 2. Of those that a mesh axis runs over, the one named last changes fastest.
Arguments:
- density: float32 [64, 512, 1024], P('depth', 'col'), may hold values from -6 to 6
- offsets: int32 [64], P('depth'), may hold values from 0 to 8, as said below
- view_flip: int32 [512], P('col'), may hold values from 0 to 1
Outputs:
- image: float32 [4, 512, 1024], P(None, ('col', 'depth'))
The draws below stay inside these ranges and needn't reach their ends.
Inputs may be any that keep to these rules, and one draw needn't show every extreme that they name: `offsets`: in every block of 8 consecutive slices (those of one device) one slice has offset 8 and another offset 0. `view_flip`: 0: slices of lower depth index lie in front for that column; 1: the reverse.
All inputs are finite; a program needn't handle non-finite values.
Results may differ from the reference program's by a relative error of at most 0.00036.
Values may be sent and summed in bfloat16 or wider, within the bound.
A program may use at most 128 MiB of HBM per device.

```python
import jax
import jax.numpy as jnp
from jax import lax

DZ = 8
H = 1024
SMAX = 8
NZ = 64
W = 512


def draw_offsets(key, part):
    first_key, second_key, third_key = jax.random.split(key, 3)
    values = jax.random.randint(first_key, (NZ,), 0, SMAX + 1)
    block_count = NZ // DZ
    high_pos = jax.random.randint(second_key, (block_count,), 0, DZ)
    low_pos = (high_pos + 1 + jax.random.randint(third_key, (block_count,), 0, DZ - 1)) % DZ
    within = jnp.arange(NZ, dtype=jnp.int32) % DZ
    block_ids = jnp.arange(NZ, dtype=jnp.int32) // DZ
    values = jnp.where(within == high_pos[block_ids], SMAX, values)
    values = jnp.where(within == low_pos[block_ids], 0, values)
    return values.astype(jnp.int32)


def with_ends(drawn, key, low, largest):
    place = [jax.random.randint(jax.random.fold_in(key, axis), (), 0, length) for axis, length in enumerate(drawn.shape)]
    main_axis = drawn.shape.index(max(drawn.shape))
    next_to = place[:main_axis] + [(place[main_axis] + 1) % drawn.shape[main_axis]] + place[main_axis + 1:]
    return drawn.at[tuple(place)].set(low).at[tuple(next_to)].set(largest)


def levels(rng, shape, cuts, smallest, largest):
    def one(dim, shards_of):
        draws = jax.random.uniform(jax.random.fold_in(jax.random.fold_in(rng, 6), dim), (shards_of,), jnp.float32, smallest / len(cuts), largest / len(cuts))
        return jnp.repeat(jnp.exp(draws), shape[dim] // shards_of).reshape((-1,) + (1,) * (len(shape) - dim - 1))

    factor_of = one(*cuts[0])
    for cut in cuts[1:]:
        factor_of = factor_of * one(*cut)
    return factor_of


def gaussian(rng, extent, spread, most, shards=(), kind=jnp.bfloat16):
    values = jax.random.normal(rng, extent, jnp.float32) * spread
    if len(shards) > 0:
        values = levels(rng, extent, shards, -0.22, 0.18) * values
    return jnp.clip(values, min=-most, max=most).astype(kind)


def setup_inputs(seed: int = 0) -> dict:
    keys = jax.random.split(jax.random.key(seed), 4)
    density = gaussian(keys[0], (NZ, W, H), 1.0, 6.0, ((0, 8), (1, 4)), jnp.float32)
    offsets = draw_offsets(jax.random.fold_in(keys[3], 71), 0)
    view_flip = with_ends(jax.random.randint(keys[2], (W,), 0, 2), jax.random.fold_in(keys[2], 1), 0, 1).astype(jnp.int32)
    return {"density": density, "offsets": offsets, "view_flip": view_flip}


def shade_cells(extended, absorb):
    center = extended[1:-1, 1:-1]
    slope_z = (extended[2:, 1:-1] - extended[:-2, 1:-1]) * 0.5
    slope_x = (extended[1:-1, 2:] - extended[1:-1, :-2]) * 0.5
    padded_y = jnp.pad(center, ((0, 0), (0, 0), (1, 1)))
    slope_y = (padded_y[..., 2:] - padded_y[..., :-2]) * 0.5
    square = slope_x * slope_x + slope_y * slope_y + slope_z * slope_z
    lambert = (0.48 * slope_x + 0.6 * slope_y + 0.64 * slope_z) / jnp.sqrt(jnp.maximum(square, 1.0))
    lighting = 0.2 + 0.8 * jnp.abs(lambert)
    center_sq = center * center
    opacity = 1.0 - jnp.exp(-absorb * center_sq * center_sq)
    weight = opacity * lighting
    red_part = weight * jax.nn.sigmoid(2.0 * center)
    green_part = weight * jax.nn.sigmoid(1.0 - center_sq)
    blue_part = weight * jax.nn.sigmoid(-2.0 * center)
    return jnp.stack([red_part, green_part, blue_part, opacity], axis=1).astype(jnp.bfloat16)

def interp_matrix(order_size):
    row_ids = jnp.arange(order_size, dtype=jnp.int32)[:, None]
    col_ids = jnp.arange(order_size, dtype=jnp.int32)[None, :]
    distance = jnp.abs(row_ids - col_ids)
    values = jnp.where(distance == 0, 0.5, jnp.where(distance == 1, 0.1875, jnp.where(distance == 2, 0.0625, 0.0)))
    return values.astype(jnp.bfloat16)

def reference(density, offsets, view_flip):
    absorb = 0.5 / NZ
    extended_all = jnp.pad(density, ((1, 1), (1, 1), (0, 0)))
    interp = interp_matrix(H).astype(jnp.float32)
    anchor = jnp.zeros((), jnp.int32)

    def advance(carried, visit):
        colour_front, colour_back, transmit = carried
        slice_pos = visit.astype(jnp.int32)
        extended = lax.dynamic_slice_in_dim(extended_all, slice_pos, 3, 0)
        shaded = shade_cells(extended, absorb)[0]
        widened = jnp.pad(shaded, ((0, 0), (SMAX, 0), (0, 0)))
        start = (SMAX - offsets[slice_pos]).astype(jnp.int32)
        sheared = lax.dynamic_slice(widened, (anchor, start, anchor), (4, W, H))
        resampled = jnp.dot(sheared.astype(jnp.float32).reshape(4 * W, H), interp, precision=lax.Precision.HIGHEST).reshape(4, W, H)
        colour_front = colour_front + transmit[None] * resampled[:3]
        colour_back = resampled[:3] + (1.0 - resampled[3])[None] * colour_back
        transmit = transmit * (1.0 - resampled[3])
        return ((colour_front, colour_back, transmit), None)
    blank = jnp.zeros((3, W, H), jnp.float32)
    initial = (blank, blank, jnp.ones((W, H), jnp.float32))
    (colour_front, colour_back, transmit), _ = lax.scan(advance, initial, jnp.arange(NZ, dtype=jnp.int32))
    colour = jnp.where(view_flip[None, :, None] == 0, colour_front, colour_back)
    return jnp.concatenate([colour, (1.0 - transmit)[None]], axis=0)
```

```python
import functools

import jax
import jax.numpy as jnp
from jax import lax
from jax.experimental import pallas as pl
from jax.experimental.pallas import tpu as pltpu
from jax.sharding import PartitionSpec as P

SMAX = 8
LEFT = SMAX + 1
SUB = 8
LANES = 128
MESH = pl.DeviceIdType.MESH
DENSITY_SCALE = 65535.0 / 12.0
IMAGE_SCALE = 65530.0


def pack(low, high):
    return low | lax.shift_left(high, jnp.full_like(high, 16))


def low_half(word):
    return (word & 0xFFFF).astype(jnp.float32)


def high_half(word):
    return lax.shift_right_logical(word, jnp.full_like(word, 16)).astype(jnp.float32)


def density_code(value):
    return ((value + 6.0) * DENSITY_SCALE + 0.5).astype(jnp.int32)


def density_value(code):
    return code * (1.0 / DENSITY_SCALE) - 6.0


def image_code(value):
    root = jnp.sqrt(jnp.sqrt(jnp.sqrt(value)))
    return (root * IMAGE_SCALE + 0.5).astype(jnp.int32)


def image_value(code):
    root = code * (1.0 / IMAGE_SCALE)
    square = root * root
    fourth = square * square
    return fourth * fourth


def kernel(
    col_count, depth_count,
    dens, offsets, flips, weights, out,
    nat, ext, zsend, zrecv, crecv, lhs0, lhs1, res, kept, ysend, yrecv, isend, irecv, final,
    in_sem, col_send, col_recv, z_send, z_recv, c_send, c_recv, y_send, y_recv, i_send, i_recv,
):
    slices, columns, height = nat.shape
    absorb = 0.5 / (slices * depth_count)
    block = columns // depth_count
    pairs = depth_count // 2
    half = columns // 2
    chunk = min(8, block)
    group = min(4, chunk)
    col = lax.axis_index("col")
    depth = lax.axis_index("depth")
    side = lax.rem(depth, 2)
    rank = depth // 2
    has_left, has_right = col > 0, col < col_count - 1
    has_up, has_down = depth > 0, depth < depth_count - 1

    def at(c, d):
        return {"col": c, "depth": d}

    order = [0, slices - 1] + list(range(1, slices - 1))
    loads = [pltpu.make_async_copy(dens.at[k], nat.at[k], in_sem.at[k]) for k in range(slices)]
    for k in order:
        loads[k].start()

    barrier = pltpu.get_barrier_semaphore()

    def greet(c, d):
        pl.semaphore_signal(barrier, inc=1, device_id=at(c, d), device_id_type=MESH)

    def greet_rank(i, carry):
        greet(col, lax.rem(rank + i, pairs) * 2 + side)
        return carry

    lax.fori_loop(1, pairs, greet_rank, 0)
    pl.when(has_up)(lambda: greet(col, depth - 1))
    pl.when(has_down)(lambda: greet(col, depth + 1))
    one = jnp.int32(1)
    none = jnp.int32(0)
    depth_sides = jnp.where(has_up, one, none) + jnp.where(has_down, one, none)
    col_sides = jnp.where(has_left, one, none) + jnp.where(has_right, one, none)
    for step, present in ((-1, has_left), (1, has_right)):
        pl.when(present)(lambda step=step: greet(col + step, depth))
        pl.when(present & has_up)(lambda step=step: greet(col + step, depth - 1))
        pl.when(present & has_down)(lambda step=step: greet(col + step, depth + 1))

    def relayout(k):
        def body(i, carry):
            x0 = pl.multiple_of(i * 8, 8)
            ext[k + 1, pl.ds(LEFT + x0, 8)] = nat[k, pl.ds(x0, 8), :].reshape(8, SUB, LANES)
            return carry

        lax.fori_loop(0, columns // 8, body, 0)

    def encode_slice(slot, k):
        def body(i, carry):
            low = ext[k + 1, pl.ds(LEFT + i * 8, 8)]
            high = ext[k + 1, pl.ds(LEFT + half + i * 8, 8)]
            zsend[slot, pl.ds(i * 8, 8)] = pack(density_code(low), density_code(high))
            return carry

        lax.fori_loop(0, half // 8, body, 0)

    for k in (0, slices - 1):
        loads[k].wait()
        relayout(k)
    encode_slice(0, slices - 1)
    encode_slice(1, 0)
    pl.semaphore_wait(barrier, pairs - 1 + depth_sides + col_sides + col_sides * depth_sides)

    def remote(src, dst, send, recv, c, d):
        return pltpu.make_async_remote_copy(
            src_ref=src, dst_ref=dst, send_sem=send, recv_sem=recv, device_id=at(c, d), device_id_type=MESH
        )

    tail = pl.ds(half - SMAX, SMAX)
    z_copies = [
        remote(zsend.at[0], zrecv.at[0], z_send.at[0], z_recv.at[0], col, depth + 1),
        remote(zsend.at[1], zrecv.at[1], z_send.at[1], z_recv.at[1], col, depth - 1),
    ]
    c_copies = [
        remote(zsend.at[0, tail], crecv.at[0], c_send.at[0], c_recv.at[0], col + 1, depth + 1),
        remote(zsend.at[1, tail], crecv.at[1], c_send.at[1], c_recv.at[1], col + 1, depth - 1),
    ]
    z_out = (has_down, has_up)
    z_in = (has_up, has_down)
    for slot in range(2):
        pl.when(z_out[slot])(z_copies[slot].start)
        pl.when(z_out[slot] & has_right)(c_copies[slot].start)

    for k in range(1, slices - 1):
        loads[k].wait()
        relayout(k)
    inner = pl.ds(1, slices)
    to_right = remote(
        ext.at[inner, pl.ds(columns, LEFT)], ext.at[inner, pl.ds(0, LEFT)],
        col_send.at[0], col_recv.at[0], col + 1, depth,
    )
    to_left = remote(
        ext.at[inner, pl.ds(LEFT, 1)], ext.at[inner, pl.ds(LEFT + columns, 1)],
        col_send.at[1], col_recv.at[1], col - 1, depth,
    )
    pl.when(has_right)(to_right.start)
    pl.when(has_left)(to_left.start)

    @pl.when(jnp.logical_not(has_left))
    def _():
        ext[:, pl.ds(0, LEFT)] = jnp.zeros((slices + 2, LEFT, SUB, LANES), jnp.float32)

    @pl.when(jnp.logical_not(has_right))
    def _():
        ext[:, pl.ds(LEFT + columns, 1)] = jnp.zeros((slices + 2, 1, SUB, LANES), jnp.float32)

    def wait_col():
        pl.when(has_right)(to_right.wait_send)
        pl.when(has_left)(to_left.wait_send)
        pl.when(has_left)(to_right.wait_recv)
        pl.when(has_right)(to_left.wait_recv)

    wait_col()

    shape = (group, SUB, LANES)
    lane = lax.broadcasted_iota(jnp.int32, shape, 2)
    sub = lax.broadcasted_iota(jnp.int32, shape, 1)
    not_first = jnp.where(sub == 0, 0.0, 1.0)
    not_last = jnp.where(sub == SUB - 1, 0.0, 1.0)
    low_lanes = lane < LANES // 2
    edge_mask = jnp.where(low_lanes, not_last, not_first)

    def shade(k, x0, lhs):
        for g in range(chunk // group):
            row = LEFT + x0 + g * group - offsets[k]
            rows = group * SUB
            window = [ext[k + 1, row + i] for i in range(-1, group + 1)]
            center = jnp.stack(window[1:-1])
            dx = jnp.stack(window[2:]) - jnp.stack(window[:-2])
            dz = jnp.stack([ext[k + 2, row + i] - ext[k, row + i] for i in range(group)])
            before = jnp.where(lane == LANES - 1, pltpu.roll(center, 1, 1) * not_first, center)
            after = jnp.where(lane == 0, pltpu.roll(center, SUB - 1, 1) * not_last, center)
            dy = pltpu.roll(after, LANES - 1, 2) - pltpu.roll(before, 1, 2)
            square = dx * dx + dy * dy + dz * dz
            lambert = (0.48 * dx + 0.6 * dy + 0.64 * dz) * lax.rsqrt(jnp.maximum(square, 4.0))
            center_sq = center * center
            opacity = 1.0 - jnp.exp(-absorb * center_sq * center_sq)
            halved = opacity * (0.1 + 0.4 * jnp.abs(lambert))
            tilt = halved * jnp.tanh(center)
            green = halved + halved * jnp.tanh(0.5 - 0.5 * center_sq)
            for ch, value in enumerate((halved + tilt, green, halved - tilt, opacity)):
                edge = jnp.where(low_lanes, pltpu.roll(value, SUB - 1, 1), pltpu.roll(value, 1, 1)) * edge_mask
                place = pl.ds((ch * chunk + g * group) * SUB, rows)
                lhs[place, 0:LANES] = value.reshape(rows, LANES).astype(jnp.bfloat16)
                lhs[place, LANES : 2 * LANES] = edge.reshape(rows, LANES).astype(jnp.bfloat16)

    def resample(k, x0, lhs):
        value = jnp.dot(lhs[...], weights[...], preferred_element_type=jnp.float32)
        res[k, :, pl.ds(x0, chunk)] = value.reshape(4, chunk, SUB, LANES)

    def inner_slice(k, carry):
        def body(i, inner_carry):
            x0 = i * 2 * chunk
            shade(k, x0, lhs0)
            resample(k, x0, lhs0)
            shade(k, x0 + chunk, lhs1)
            resample(k, x0 + chunk, lhs1)
            return inner_carry

        return lax.fori_loop(0, columns // (2 * chunk), body, carry)

    lax.fori_loop(1, slices - 1, inner_slice, 0)

    def decode_slice(slot, plane):
        def body(i, carry):
            word = zrecv[slot, pl.ds(i * 8, 8)]
            ext[plane, pl.ds(LEFT + i * 8, 8)] = density_value(low_half(word))
            ext[plane, pl.ds(LEFT + half + i * 8, 8)] = density_value(high_half(word))
            return carry

        lax.fori_loop(0, half // 8, body, 0)

    for slot, plane in ((0, 0), (1, slices + 1)):
        @pl.when(z_in[slot])
        def _(slot=slot, plane=plane):
            z_copies[slot].wait_recv()
            decode_slice(slot, plane)

        @pl.when(z_in[slot] & has_left)
        def _(slot=slot, plane=plane):
            c_copies[slot].wait_recv()
            ext[plane, pl.ds(1, SMAX)] = density_value(high_half(crecv[slot]))

        @pl.when(jnp.logical_not(z_in[slot]))
        def _(plane=plane):
            ext[plane] = jnp.zeros(ext.shape[1:], jnp.float32)

    def finish_block(number):
        start = number * block
        for i in range(block // chunk):
            shade(0, start + i * chunk, lhs0)
            resample(0, start + i * chunk, lhs0)
            shade(slices - 1, start + i * chunk, lhs1)
            resample(slices - 1, start + i * chunk, lhs1)

    def column_partial(x):
        flip = flips[x]
        colour = [None] * 3
        transmit = None
        for i in range(slices):
            k = i + flip * (slices - 1 - 2 * i)
            through = 1.0 - res[k, 3, x]
            for ch in range(3):
                value = res[k, ch, x]
                colour[ch] = value if i == 0 else colour[ch] + transmit * value
            transmit = through if i == 0 else transmit * through
        return colour, transmit

    def store_codes(ref, slot, x, colour, opacity):
        ref[slot, 0, x] = pack(image_code(colour[0]), image_code(colour[1]))
        ref[slot, 1, x] = pack(image_code(colour[2]), image_code(opacity))

    def load_codes(first, second):
        colour = [image_value(low_half(first)), image_value(high_half(first)), image_value(low_half(second))]
        return colour, image_value(high_half(second))

    def y_copy(slot):
        return remote(ysend.at[slot], yrecv.at[slot], y_send.at[slot], y_recv.at[slot], col, depth + 1 - 2 * side)

    def i_copy(slot):
        return remote(isend.at[slot], irecv.at[rank], i_send.at[slot], i_recv.at[rank], col, 2 * slot + side)

    def give(i, carry):
        slot = lax.rem(rank + 1 + i, pairs)
        number = 2 * slot + 1 - side
        finish_block(number)

        def body(x, inner_carry):
            colour, transmit = column_partial(number * block + x)
            store_codes(ysend, slot, x, colour, 1.0 - transmit)
            return inner_carry

        lax.fori_loop(0, block, body, 0)
        y_copy(slot).start()
        return carry

    lax.fori_loop(0, pairs, give, 0)

    def keep(i, carry):
        slot = lax.rem(rank + 1 + i, pairs)
        number = 2 * slot + side
        finish_block(number)

        def body(x, inner_carry):
            colour, transmit = column_partial(number * block + x)
            for ch in range(3):
                kept[ch, x] = colour[ch]
            kept[3, x] = transmit
            return inner_carry

        lax.fori_loop(0, block, body, 0)
        y_copy(slot).wait_recv()

        def join(x, inner_carry):
            theirs, their_opacity = load_codes(yrecv[slot, 0, x], yrecv[slot, 1, x])
            their_transmit = 1.0 - their_opacity
            mine = [kept[ch, x] for ch in range(3)]
            my_transmit = kept[3, x]
            mine_first = jnp.full((SUB, LANES), flips[number * block + x], jnp.int32) == side
            front_transmit = jnp.where(mine_first, my_transmit, their_transmit)
            colour = []
            for ch in range(3):
                front = jnp.where(mine_first, mine[ch], theirs[ch])
                behind = jnp.where(mine_first, theirs[ch], mine[ch])
                colour.append(front + front_transmit * behind)
            opacity = 1.0 - my_transmit * their_transmit

            @pl.when(i < pairs - 1)
            def _():
                store_codes(isend, slot, x, colour, opacity)

            @pl.when(i == pairs - 1)
            def _():
                store_codes(irecv, rank, x, colour, opacity)

            return inner_carry

        lax.fori_loop(0, block, join, 0)
        pl.when(i < pairs - 1)(lambda: i_copy(slot).start())
        return carry

    lax.fori_loop(0, pairs, keep, 0)

    def arrive(i, carry):
        slot = lax.rem(rank + i, pairs)
        remote(
            isend.at[slot], irecv.at[slot], i_send.at[slot], i_recv.at[slot], col, 2 * slot + side
        ).wait_recv()
        return carry

    lax.fori_loop(1, pairs, arrive, 0)

    def compose(x, carry):
        flip = flips[depth * block + x]
        colour = [None] * 3
        transmit = None
        for i in range(pairs):
            slot = i + flip * (pairs - 1 - 2 * i)
            value, opacity = load_codes(irecv[slot, 0, x], irecv[slot, 1, x])
            for ch in range(3):
                colour[ch] = value[ch] if i == 0 else colour[ch] + transmit * value[ch]
            transmit = 1.0 - opacity if i == 0 else transmit * (1.0 - opacity)
        for ch in range(3):
            final[ch, x] = colour[ch]
        final[3, x] = 1.0 - transmit
        return carry

    lax.fori_loop(0, block, compose, 0)
    part = min(8, block)
    for ch in range(4):
        for x0 in range(0, block, part):
            out[ch, x0 : x0 + part, :] = final[ch, x0 : x0 + part].reshape(part, height)

    for slot in range(2):
        pl.when(z_out[slot])(z_copies[slot].wait_send)
        pl.when(z_out[slot] & has_right)(c_copies[slot].wait_send)

    def left_y(i, carry):
        y_copy(i).wait_send()
        return carry

    lax.fori_loop(0, pairs, left_y, 0)

    def left_i(i, carry):
        i_copy(lax.rem(rank + i, pairs)).wait_send()
        return carry

    lax.fori_loop(1, pairs, left_i, 0)


def resample_weights():
    source = jnp.arange(LANES, dtype=jnp.int32)[:, None]
    target = jnp.arange(LANES, dtype=jnp.int32)[None, :]

    def taps(distance):
        distance = jnp.abs(distance)
        return jnp.where(distance == 0, 0.5, jnp.where(distance == 1, 0.1875, jnp.where(distance == 2, 0.0625, 0.0)))

    own = taps(source - target)
    beside = jnp.where(source < LANES // 2, taps(source + LANES - target), taps(source - LANES - target))
    return jnp.concatenate([own, beside], axis=0).astype(jnp.bfloat16)


def on_device(density, offsets, view_flip):
    col_count, depth_count = lax.axis_size("col"), lax.axis_size("depth")
    slices, columns, height = density.shape
    block = columns // depth_count
    pairs = depth_count // 2
    chunk = min(8, block)
    half = columns // 2
    f32, i32 = jnp.float32, jnp.int32
    dma = pltpu.SemaphoreType.DMA
    image = pltpu.VMEM((pairs, 2, block, SUB, LANES), i32)
    scratch = [
        pltpu.VMEM((slices, columns, height), f32),
        pltpu.VMEM((slices + 2, LEFT + columns + 1, SUB, LANES), f32),
        pltpu.VMEM((2, half, SUB, LANES), i32),
        pltpu.VMEM((2, half, SUB, LANES), i32),
        pltpu.VMEM((2, SMAX, SUB, LANES), i32),
        pltpu.VMEM((4 * chunk * SUB, 2 * LANES), jnp.bfloat16),
        pltpu.VMEM((4 * chunk * SUB, 2 * LANES), jnp.bfloat16),
        pltpu.VMEM((slices, 4, columns, SUB, LANES), f32),
        pltpu.VMEM((4, block, SUB, LANES), f32),
        image, image, image, image,
        pltpu.VMEM((4, block, SUB, LANES), f32),
        dma((slices,)),
        dma((2,)), dma((2,)), dma((2,)), dma((2,)), dma((2,)), dma((2,)),
        dma((pairs,)), dma((pairs,)), dma((pairs,)), dma((pairs,)),
    ]
    vmem = pl.BlockSpec(memory_space=pltpu.VMEM)
    smem = pl.BlockSpec(memory_space=pltpu.SMEM)
    return pl.pallas_call(
        functools.partial(kernel, col_count, depth_count),
        out_shape=jax.ShapeDtypeStruct((4, block, height), f32),
        in_specs=[pl.BlockSpec(memory_space=pl.ANY), smem, smem, vmem],
        out_specs=vmem,
        scratch_shapes=scratch,
        compiler_params=pltpu.CompilerParams(
            collective_id=0, has_side_effects=True, vmem_limit_bytes=48 * 2**20
        ),
    )(density, offsets, view_flip, resample_weights())


def solution(mesh):
    in_specs = (P("depth", "col", None), P("depth"), P("col"))
    out_specs = P(None, ("col", "depth"), None)
    return jax.shard_map(
        on_device, mesh=mesh, in_specs=in_specs, out_specs=out_specs, check_vma=False
    )
```

```python
import functools

import jax
import jax.numpy as jnp
from jax import lax
from jax.experimental import pallas as pl
from jax.experimental.pallas import tpu as pltpu
from jax.sharding import PartitionSpec as P

SMAX = 8
LEFT = SMAX + 1
SUB = 8
LANES = 128
MESH = pl.DeviceIdType.MESH
DENSITY_SCALE = 65535.0 / 12.0
IMAGE_SCALE = 65530.0


def pack(low, high):
    return low | lax.shift_left(high, jnp.full_like(high, 16))


def low_half(word):
    return (word & 0xFFFF).astype(jnp.float32)


def high_half(word):
    return lax.shift_right_logical(word, jnp.full_like(word, 16)).astype(jnp.float32)


def density_code(value):
    return ((value + 6.0) * DENSITY_SCALE + 0.5).astype(jnp.int32)


def density_value(code):
    return code * (1.0 / DENSITY_SCALE) - 6.0


def image_code(value):
    root = jnp.sqrt(jnp.sqrt(jnp.sqrt(value)))
    return (root * IMAGE_SCALE + 0.5).astype(jnp.int32)


def image_value(code):
    root = code * (1.0 / IMAGE_SCALE)
    square = root * root
    fourth = square * square
    return fourth * fourth


def kernel(
    col_count, depth_count,
    dens, offsets_in, flips_in, out,
    offsets, flips, weights, nat, ext, lrecv, rrecv, zsend, zrecv, crecv, lhs0, lhs1, res, kept,
    ysend, yrecv, isend, irecv, final, small_sem, in_sem, col_send, col_recv, z_send, z_recv, c_send, c_recv, y_send, y_recv, i_send, i_recv,
):
    slices, columns, height = nat.shape
    absorb = 0.5 / (slices * depth_count)
    block = columns // depth_count
    pairs = depth_count // 2
    half = columns // 2
    chunk = min(16, block)
    group = min(4, chunk)
    lump = min(4, block)
    col = lax.axis_index("col")
    depth = lax.axis_index("depth")
    side = lax.rem(depth, 2)
    rank = depth // 2
    has_left, has_right = col > 0, col < col_count - 1
    has_up, has_down = depth > 0, depth < depth_count - 1

    def at(c, d):
        return {"col": c, "depth": d}

    order = [0, slices - 1] + list(range(1, slices - 1))
    loads = [pltpu.make_async_copy(dens.at[k], nat.at[k], in_sem.at[k]) for k in range(slices)]
    for k in order:
        loads[k].start()

    small = [
        pltpu.make_async_copy(offsets_in, offsets, small_sem.at[0]),
        pltpu.make_async_copy(flips_in, flips, small_sem.at[1]),
    ]
    for load in small:
        load.start()

    barrier = pltpu.get_barrier_semaphore()

    def greet(c, d):
        pl.semaphore_signal(barrier, inc=1, device_id=at(c, d), device_id_type=MESH)

    def greet_rank(i, carry):
        greet(col, lax.rem(rank + i, pairs) * 2 + side)
        return carry

    lax.fori_loop(1, pairs, greet_rank, 0)
    pl.when(has_up)(lambda: greet(col, depth - 1))
    pl.when(has_down)(lambda: greet(col, depth + 1))
    one = jnp.int32(1)
    none = jnp.int32(0)
    depth_sides = jnp.where(has_up, one, none) + jnp.where(has_down, one, none)
    col_sides = jnp.where(has_left, one, none) + jnp.where(has_right, one, none)
    for step, present in ((-1, has_left), (1, has_right)):
        pl.when(present)(lambda step=step: greet(col + step, depth))
        pl.when(present & has_up)(lambda step=step: greet(col + step, depth - 1))
        pl.when(present & has_down)(lambda step=step: greet(col + step, depth + 1))

    def move(k, x0):
        ext[k + 1, pl.ds(LEFT + x0, 8)] = nat[k, pl.ds(x0, 8), :].reshape(8, SUB, LANES)

    def relayout(k):
        def body(i, carry):
            for u in range(4):
                move(k, pl.multiple_of(i * 32 + u * 8, 8))
            return carry

        lax.fori_loop(0, columns // 32, body, 0)

    def encode_slice(slot, k):
        def body(i, carry):
            low = ext[k + 1, pl.ds(LEFT + i * 8, 8)]
            high = ext[k + 1, pl.ds(LEFT + half + i * 8, 8)]
            zsend[slot, pl.ds(i * 8, 8)] = pack(density_code(low), density_code(high))
            return carry

        lax.fori_loop(0, half // 8, body, 0)

    for k in (0, slices - 1):
        loads[k].wait()
        relayout(k)
    encode_slice(0, slices - 1)
    encode_slice(1, 0)
    pl.semaphore_wait(barrier, pairs - 1 + depth_sides + col_sides + col_sides * depth_sides)

    def remote(src, dst, send, recv, c, d):
        return pltpu.make_async_remote_copy(
            src_ref=src, dst_ref=dst, send_sem=send, recv_sem=recv, device_id=at(c, d), device_id_type=MESH
        )

    tail = pl.ds(half - SMAX, SMAX)
    z_copies = [
        remote(zsend.at[0], zrecv.at[0], z_send.at[0], z_recv.at[0], col, depth + 1),
        remote(zsend.at[1], zrecv.at[1], z_send.at[1], z_recv.at[1], col, depth - 1),
    ]
    c_copies = [
        remote(zsend.at[0, tail], crecv.at[0], c_send.at[0], c_recv.at[0], col + 1, depth + 1),
        remote(zsend.at[1, tail], crecv.at[1], c_send.at[1], c_recv.at[1], col + 1, depth - 1),
    ]
    z_out = (has_down, has_up)
    z_in = (has_up, has_down)
    for slot in range(2):
        pl.when(z_out[slot])(z_copies[slot].start)
        pl.when(z_out[slot] & has_right)(c_copies[slot].start)

    for k in range(1, slices - 1):
        loads[k].wait()
        for x0 in (0, columns - 16, columns - 8):
            move(k, x0)
    inner = pl.ds(1, slices)
    to_right = remote(ext.at[inner, pl.ds(columns, LEFT)], lrecv, col_send.at[0], col_recv.at[0], col + 1, depth)
    to_left = remote(ext.at[inner, pl.ds(LEFT, 1)], rrecv, col_send.at[1], col_recv.at[1], col - 1, depth)
    pl.when(has_right)(to_right.start)
    pl.when(has_left)(to_left.start)

    def relayout_inner(k, carry):
        def body(i, inner_carry):
            for u in range(4):
                move(k, pl.multiple_of(8 + jnp.minimum(i * 32 + u * 8, columns - 32), 8))
            return inner_carry

        return lax.fori_loop(0, columns // 32, body, carry)

    lax.fori_loop(1, slices - 1, relayout_inner, 0)

    source = lax.broadcasted_iota(jnp.int32, (LANES, LANES), 0)
    target = lax.broadcasted_iota(jnp.int32, (LANES, LANES), 1)

    def taps(distance):
        distance = jnp.abs(distance)
        return jnp.where(distance == 0, 0.5, jnp.where(distance == 1, 0.1875, jnp.where(distance == 2, 0.0625, 0.0)))

    weights[0:LANES, :] = taps(source - target).astype(jnp.bfloat16)
    shift = jnp.where(source < LANES // 2, LANES, -LANES)
    weights[LANES : 2 * LANES, :] = taps(source + shift - target).astype(jnp.bfloat16)
    for load in small:
        load.wait()

    shape = (group, SUB, LANES)
    lane = lax.broadcasted_iota(jnp.int32, shape, 2)
    sub = lax.broadcasted_iota(jnp.int32, shape, 1)
    not_first = jnp.where(sub == 0, 0.0, 1.0)
    not_last = jnp.where(sub == SUB - 1, 0.0, 1.0)
    low_lanes = lane < LANES // 2
    edge_mask = jnp.where(low_lanes, not_last, not_first)

    def shade(k, x0, lhs):
        for g in range(chunk // group):
            row = LEFT + x0 + g * group - offsets[k]
            rows = group * SUB
            window = [ext[k + 1, row + i] for i in range(-1, group + 1)]
            center = jnp.stack(window[1:-1])
            dx = jnp.stack(window[2:]) - jnp.stack(window[:-2])
            dz = jnp.stack([ext[k + 2, row + i] - ext[k, row + i] for i in range(group)])
            before = jnp.where(lane == LANES - 1, pltpu.roll(center, 1, 1) * not_first, center)
            after = jnp.where(lane == 0, pltpu.roll(center, SUB - 1, 1) * not_last, center)
            dy = pltpu.roll(after, LANES - 1, 2) - pltpu.roll(before, 1, 2)
            square = dx * dx + dy * dy + dz * dz
            lambert = (0.48 * dx + 0.6 * dy + 0.64 * dz) * lax.rsqrt(jnp.maximum(square, 4.0))
            center_sq = center * center
            opacity = 1.0 - jnp.exp(-absorb * center_sq * center_sq)
            halved = opacity * (0.1 + 0.4 * jnp.abs(lambert))
            tilt = halved * jnp.tanh(center)
            green = halved + halved * jnp.tanh(0.5 - 0.5 * center_sq)
            for ch, value in enumerate((halved + tilt, green, halved - tilt, opacity)):
                edge = jnp.where(low_lanes, pltpu.roll(value, SUB - 1, 1), pltpu.roll(value, 1, 1)) * edge_mask
                place = pl.ds((ch * chunk + g * group) * SUB, rows)
                lhs[place, 0:LANES] = value.reshape(rows, LANES).astype(jnp.bfloat16)
                lhs[place, LANES : 2 * LANES] = edge.reshape(rows, LANES).astype(jnp.bfloat16)

    def resample(k, x0, lhs):
        value = jnp.dot(lhs[...], weights[...], preferred_element_type=jnp.float32)
        res[k, :, pl.ds(x0, chunk)] = value.reshape(4, chunk, SUB, LANES)

    def run(count, place):
        shade(*place(0), lhs0)

        def pair(i, last):
            resample(*place(2 * i), lhs0)
            shade(*place(2 * i + 1), lhs1)
            resample(*place(2 * i + 1), lhs1)
            if not last:
                shade(*place(2 * i + 2), lhs0)

        def body(i, carry):
            pair(i, False)
            return carry

        lax.fori_loop(0, count // 2 - 1, body, 0)
        pair(count // 2 - 1, True)

    chunks = columns // chunk
    left_chunks = -(-LEFT // chunk)
    mid_chunks = chunks - left_chunks - 1
    rim_chunks = left_chunks + 1
    mid_slices = slices - 2

    def mid_place(t):
        t = jnp.int32(t)
        return 1 + t // mid_chunks, (left_chunks + lax.rem(t, mid_chunks)) * chunk

    def rim_place(t):
        t = jnp.int32(t)
        return 1 + t // rim_chunks, lax.rem(chunks - 1 + lax.rem(t, rim_chunks), chunks) * chunk

    run(mid_slices * mid_chunks, mid_place)

    pl.when(has_right)(to_right.wait_send)
    pl.when(has_left)(to_left.wait_send)

    @pl.when(has_left)
    def _():
        to_right.wait_recv()
        ext[1 : slices + 1, 0:LEFT] = lrecv[...]

    @pl.when(has_right)
    def _():
        to_left.wait_recv()
        ext[1 : slices + 1, LEFT + columns : LEFT + columns + 1] = rrecv[...]

    @pl.when(jnp.logical_not(has_left))
    def _():
        ext[:, 0:LEFT] = jnp.zeros((slices + 2, LEFT, SUB, LANES), jnp.float32)

    @pl.when(jnp.logical_not(has_right))
    def _():
        ext[:, LEFT + columns : LEFT + columns + 1] = jnp.zeros((slices + 2, 1, SUB, LANES), jnp.float32)

    run(mid_slices * rim_chunks, rim_place)

    def decode_slice(slot, plane):
        def body(i, carry):
            word = zrecv[slot, pl.ds(i * 8, 8)]
            ext[plane, pl.ds(LEFT + i * 8, 8)] = density_value(low_half(word))
            ext[plane, pl.ds(LEFT + half + i * 8, 8)] = density_value(high_half(word))
            return carry

        lax.fori_loop(0, half // 8, body, 0)

    for slot, plane in ((0, 0), (1, slices + 1)):
        @pl.when(z_in[slot])
        def _(slot=slot, plane=plane):
            z_copies[slot].wait_recv()
            decode_slice(slot, plane)

        @pl.when(z_in[slot] & has_left)
        def _(slot=slot, plane=plane):
            c_copies[slot].wait_recv()
            ext[plane, pl.ds(1, SMAX)] = density_value(high_half(crecv[slot]))

        @pl.when(jnp.logical_not(z_in[slot]))
        def _(plane=plane):
            ext[plane] = jnp.zeros(ext.shape[1:], jnp.float32)

    def finish_block(number):
        start = number * block
        for i in range(block // chunk):
            shade(0, start + i * chunk, lhs0)
            resample(0, start + i * chunk, lhs0)
            shade(slices - 1, start + i * chunk, lhs1)
            resample(slices - 1, start + i * chunk, lhs1)

    def column_partial(x):
        flip = [flips[x + u] for u in range(lump)]
        colour = [None] * 3
        transmit = None
        for i in range(slices):
            depths = [i + flip[u] * (slices - 1 - 2 * i) for u in range(lump)]
            through = 1.0 - jnp.stack([res[depths[u], 3, x + u] for u in range(lump)])
            for ch in range(3):
                value = jnp.stack([res[depths[u], ch, x + u] for u in range(lump)])
                colour[ch] = value if i == 0 else colour[ch] + transmit * value
            transmit = through if i == 0 else transmit * through
        return colour, transmit

    def store_codes(ref, slot, x, colour, opacity):
        span = pl.ds(x, lump)
        ref[slot, 0, span] = pack(image_code(colour[0]), image_code(colour[1]))
        ref[slot, 1, span] = pack(image_code(colour[2]), image_code(opacity))

    def load_codes(first, second):
        colour = [image_value(low_half(first)), image_value(high_half(first)), image_value(low_half(second))]
        return colour, image_value(high_half(second))

    def y_copy(slot):
        return remote(ysend.at[slot], yrecv.at[slot], y_send.at[slot], y_recv.at[slot], col, depth + 1 - 2 * side)

    def i_copy(slot):
        return remote(isend.at[slot], irecv.at[rank], i_send.at[slot], i_recv.at[rank], col, 2 * slot + side)

    def give(i, carry):
        slot = lax.rem(rank + 1 + i, pairs)
        number = 2 * slot + 1 - side
        finish_block(number)

        def body(step, inner_carry):
            x = step * lump
            colour, transmit = column_partial(number * block + x)
            store_codes(ysend, slot, x, colour, 1.0 - transmit)
            return inner_carry

        lax.fori_loop(0, block // lump, body, 0)
        y_copy(slot).start()
        return carry

    lax.fori_loop(0, pairs, give, 0)

    def keep(i, carry):
        slot = lax.rem(rank + 1 + i, pairs)
        number = 2 * slot + side
        finish_block(number)

        def body(step, inner_carry):
            x = step * lump
            colour, transmit = column_partial(number * block + x)
            for ch in range(3):
                kept[ch, pl.ds(x, lump)] = colour[ch]
            kept[3, pl.ds(x, lump)] = transmit
            return inner_carry

        lax.fori_loop(0, block // lump, body, 0)
        y_copy(slot).wait_recv()

        def join(step, inner_carry):
            x = step * lump
            span = pl.ds(x, lump)
            theirs, their_opacity = load_codes(yrecv[slot, 0, span], yrecv[slot, 1, span])
            their_transmit = 1.0 - their_opacity
            mine = [kept[ch, span] for ch in range(3)]
            my_transmit = kept[3, span]
            flip = [jnp.full((SUB, LANES), flips[number * block + x + u], jnp.int32) for u in range(lump)]
            mine_first = jnp.stack(flip) == side
            front_transmit = jnp.where(mine_first, my_transmit, their_transmit)
            colour = []
            for ch in range(3):
                front = jnp.where(mine_first, mine[ch], theirs[ch])
                behind = jnp.where(mine_first, theirs[ch], mine[ch])
                colour.append(front + front_transmit * behind)
            opacity = 1.0 - my_transmit * their_transmit

            @pl.when(i < pairs - 1)
            def _():
                store_codes(isend, slot, x, colour, opacity)

            @pl.when(i == pairs - 1)
            def _():
                store_codes(irecv, rank, x, colour, opacity)

            return inner_carry

        lax.fori_loop(0, block // lump, join, 0)
        pl.when(i < pairs - 1)(lambda: i_copy(slot).start())
        return carry

    lax.fori_loop(0, pairs, keep, 0)

    def arrive(i, carry):
        slot = lax.rem(rank + i, pairs)
        remote(
            isend.at[slot], irecv.at[slot], i_send.at[slot], i_recv.at[slot], col, 2 * slot + side
        ).wait_recv()
        return carry

    lax.fori_loop(1, pairs, arrive, 0)

    def compose(step, carry):
        x = step * lump
        flip = [flips[depth * block + x + u] for u in range(lump)]
        colour = [None] * 3
        transmit = None
        for i in range(pairs):
            slot = [i + flip[u] * (pairs - 1 - 2 * i) for u in range(lump)]
            words = [jnp.stack([irecv[slot[u], part, x + u] for u in range(lump)]) for part in range(2)]
            value, opacity = load_codes(*words)
            for ch in range(3):
                colour[ch] = value[ch] if i == 0 else colour[ch] + transmit * value[ch]
            transmit = 1.0 - opacity if i == 0 else transmit * (1.0 - opacity)
        for ch in range(3):
            final[ch, pl.ds(x, lump)] = colour[ch]
        final[3, pl.ds(x, lump)] = 1.0 - transmit
        return carry

    lax.fori_loop(0, block // lump, compose, 0)
    part = min(8, block)
    for ch in range(4):
        for x0 in range(0, block, part):
            out[ch, x0 : x0 + part, :] = final[ch, x0 : x0 + part].reshape(part, height)

    for slot in range(2):
        pl.when(z_out[slot])(z_copies[slot].wait_send)
        pl.when(z_out[slot] & has_right)(c_copies[slot].wait_send)

    def left_y(i, carry):
        y_copy(i).wait_send()
        return carry

    lax.fori_loop(0, pairs, left_y, 0)

    def left_i(i, carry):
        i_copy(lax.rem(rank + i, pairs)).wait_send()
        return carry

    lax.fori_loop(1, pairs, left_i, 0)


def on_device(density, offsets, view_flip):
    col_count, depth_count = lax.axis_size("col"), lax.axis_size("depth")
    slices, columns, height = density.shape
    block = columns // depth_count
    pairs = depth_count // 2
    chunk = min(16, block)
    half = columns // 2
    f32, i32 = jnp.float32, jnp.int32
    dma = pltpu.SemaphoreType.DMA
    image = pltpu.VMEM((pairs, 2, block, SUB, LANES), i32)
    scratch = [
        pltpu.SMEM((slices,), i32),
        pltpu.SMEM((columns,), i32),
        pltpu.VMEM((2 * LANES, LANES), jnp.bfloat16),
        pltpu.VMEM((slices, columns, height), f32),
        pltpu.VMEM((slices + 2, LEFT + columns + 1, SUB, LANES), f32),
        pltpu.VMEM((slices, LEFT, SUB, LANES), f32),
        pltpu.VMEM((slices, 1, SUB, LANES), f32),
        pltpu.VMEM((2, half, SUB, LANES), i32),
        pltpu.VMEM((2, half, SUB, LANES), i32),
        pltpu.VMEM((2, SMAX, SUB, LANES), i32),
        pltpu.VMEM((4 * chunk * SUB, 2 * LANES), jnp.bfloat16),
        pltpu.VMEM((4 * chunk * SUB, 2 * LANES), jnp.bfloat16),
        pltpu.VMEM((slices, 4, columns, SUB, LANES), f32),
        pltpu.VMEM((4, block, SUB, LANES), f32),
        image, image, image, image,
        pltpu.VMEM((4, block, SUB, LANES), f32),
        dma((2,)),
        dma((slices,)),
        dma((2,)), dma((2,)), dma((2,)), dma((2,)), dma((2,)), dma((2,)),
        dma((pairs,)), dma((pairs,)), dma((pairs,)), dma((pairs,)),
    ]
    vmem = pl.BlockSpec(memory_space=pltpu.VMEM)
    hbm = pl.BlockSpec(memory_space=pltpu.HBM)
    return pl.pallas_call(
        functools.partial(kernel, col_count, depth_count),
        out_shape=jax.ShapeDtypeStruct((4, block, height), f32),
        in_specs=[hbm, hbm, hbm],
        out_specs=vmem,
        scratch_shapes=scratch,
        compiler_params=pltpu.CompilerParams(
            collective_id=0, has_side_effects=True, vmem_limit_bytes=48 * 2**20
        ),
    )(density, offsets, view_flip)


def solution(mesh):
    in_specs = (P("depth", "col", None), P("depth"), P("col"))
    out_specs = P(None, ("col", "depth"), None)
    return jax.shard_map(
        on_device, mesh=mesh, in_specs=in_specs, out_specs=out_specs, check_vma=False
    )
```

```python
import functools

import jax
import jax.numpy as jnp
from jax import lax
from jax.experimental import pallas as pl
from jax.experimental.pallas import tpu as pltpu
from jax.sharding import PartitionSpec as P

SMAX = 8
LEFT = SMAX + 1
SUB = 8
LANES = 128
MESH = pl.DeviceIdType.MESH
DENSITY_SCALE = 65535.0 / 12.0
IMAGE_SCALE = 65530.0


def pack(low, high):
    return low | lax.shift_left(high, jnp.full_like(high, 16))


def low_half(word):
    return (word & 0xFFFF).astype(jnp.float32)


def high_half(word):
    return lax.shift_right_logical(word, jnp.full_like(word, 16)).astype(jnp.float32)


def density_code(value):
    return ((value + 6.0) * DENSITY_SCALE + 0.5).astype(jnp.int32)


def density_value(code):
    return code * (1.0 / DENSITY_SCALE) - 6.0


def image_code(value):
    root = jnp.sqrt(jnp.sqrt(jnp.sqrt(value)))
    return (root * IMAGE_SCALE + 0.5).astype(jnp.int32)


def image_value(code):
    root = code * (1.0 / IMAGE_SCALE)
    square = root * root
    fourth = square * square
    return fourth * fourth


def kernel(
    col_count, depth_count,
    dens, offsets_in, flips_in, out,
    offsets, flips, weights, ext, lrecv, rrecv, zsend, zrecv, crecv, lhs0, lhs1, res, kept,
    ysend, yrecv, isend, irecv, final, small_sem, in_sem, col_send, col_recv, z_send, z_recv, c_send, c_recv, y_send, y_recv, i_send, i_recv,
):
    slices, columns, height = dens.shape
    absorb = 0.5 / (slices * depth_count)
    block = columns // depth_count
    pairs = depth_count // 2
    half = columns // 2
    group = min(4, block)
    lump = min(4, block)
    col = lax.axis_index("col")
    depth = lax.axis_index("depth")
    side = lax.rem(depth, 2)
    rank = depth // 2
    has_left, has_right = col > 0, col < col_count - 1
    has_up, has_down = depth > 0, depth < depth_count - 1

    def at(c, d):
        return {"col": c, "depth": d}

    def load(k, s):
        return pltpu.make_async_copy(
            dens.at[k, :, pl.ds(s * LANES, LANES)], ext.at[k + 1, pl.ds(LEFT, columns), s], in_sem.at[k, s]
        )

    for k in [0, slices - 1] + list(range(1, slices - 1)):
        for s in range(SUB):
            load(k, s).start()

    small = [
        pltpu.make_async_copy(offsets_in, offsets, small_sem.at[0]),
        pltpu.make_async_copy(flips_in, flips, small_sem.at[1]),
    ]
    for copy in small:
        copy.start()

    barrier = pltpu.get_barrier_semaphore()

    def greet(c, d):
        pl.semaphore_signal(barrier, inc=1, device_id=at(c, d), device_id_type=MESH)

    def greet_rank(i, carry):
        greet(col, lax.rem(rank + i, pairs) * 2 + side)
        return carry

    lax.fori_loop(1, pairs, greet_rank, 0)
    pl.when(has_up)(lambda: greet(col, depth - 1))
    pl.when(has_down)(lambda: greet(col, depth + 1))
    one = jnp.int32(1)
    none = jnp.int32(0)
    depth_sides = jnp.where(has_up, one, none) + jnp.where(has_down, one, none)
    col_sides = jnp.where(has_left, one, none) + jnp.where(has_right, one, none)
    for step, present in ((-1, has_left), (1, has_right)):
        pl.when(present)(lambda step=step: greet(col + step, depth))
        pl.when(present & has_up)(lambda step=step: greet(col + step, depth - 1))
        pl.when(present & has_down)(lambda step=step: greet(col + step, depth + 1))

    def encode_slice(slot, k):
        def body(i, carry):
            low = ext[k + 1, pl.ds(LEFT + i * 8, 8)]
            high = ext[k + 1, pl.ds(LEFT + half + i * 8, 8)]
            zsend[slot, pl.ds(i * 8, 8)] = pack(density_code(low), density_code(high))
            return carry

        lax.fori_loop(0, half // 8, body, 0)

    for k in (0, slices - 1):
        for s in range(SUB):
            load(k, s).wait()
    encode_slice(0, slices - 1)
    encode_slice(1, 0)
    pl.semaphore_wait(barrier, pairs - 1 + depth_sides + col_sides + col_sides * depth_sides)

    def remote(src, dst, send, recv, c, d):
        return pltpu.make_async_remote_copy(
            src_ref=src, dst_ref=dst, send_sem=send, recv_sem=recv, device_id=at(c, d), device_id_type=MESH
        )

    tail = pl.ds(half - SMAX, SMAX)
    z_copies = [
        remote(zsend.at[0], zrecv.at[0], z_send.at[0], z_recv.at[0], col, depth + 1),
        remote(zsend.at[1], zrecv.at[1], z_send.at[1], z_recv.at[1], col, depth - 1),
    ]
    c_copies = [
        remote(zsend.at[0, tail], crecv.at[0], c_send.at[0], c_recv.at[0], col + 1, depth + 1),
        remote(zsend.at[1, tail], crecv.at[1], c_send.at[1], c_recv.at[1], col + 1, depth - 1),
    ]
    z_out = (has_down, has_up)
    z_in = (has_up, has_down)
    for slot in range(2):
        pl.when(z_out[slot])(z_copies[slot].start)
        pl.when(z_out[slot] & has_right)(c_copies[slot].start)

    for k in range(1, slices - 1):
        for s in range(SUB):
            load(k, s).wait()
    inner = pl.ds(1, slices)
    to_right = remote(ext.at[inner, pl.ds(columns, LEFT)], lrecv, col_send.at[0], col_recv.at[0], col + 1, depth)
    to_left = remote(ext.at[inner, pl.ds(LEFT, 1)], rrecv, col_send.at[1], col_recv.at[1], col - 1, depth)
    pl.when(has_right)(to_right.start)
    pl.when(has_left)(to_left.start)

    source = lax.broadcasted_iota(jnp.int32, (LANES, LANES), 0)
    target = lax.broadcasted_iota(jnp.int32, (LANES, LANES), 1)

    def taps(distance):
        distance = jnp.abs(distance)
        return jnp.where(distance == 0, 0.5, jnp.where(distance == 1, 0.1875, jnp.where(distance == 2, 0.0625, 0.0)))

    weights[0:LANES, :] = taps(source - target).astype(jnp.bfloat16)
    shift = jnp.where(source < LANES // 2, LANES, -LANES)
    weights[LANES : 2 * LANES, :] = taps(source + shift - target).astype(jnp.bfloat16)
    for copy in small:
        copy.wait()

    shape = (group, SUB, LANES)
    lane = lax.broadcasted_iota(jnp.int32, shape, 2)
    sub = lax.broadcasted_iota(jnp.int32, shape, 1)
    not_first = jnp.where(sub == 0, 0.0, 1.0)
    not_last = jnp.where(sub == SUB - 1, 0.0, 1.0)
    low_lanes = lane < LANES // 2
    edge_mask = jnp.where(low_lanes, not_last, not_first)

    def shade(k, x0, lhs):
        for g in range(block // group):
            row = LEFT + x0 + g * group - offsets[k]
            rows = group * SUB
            window = [ext[k + 1, row + i] for i in range(-1, group + 1)]
            center = jnp.stack(window[1:-1])
            dx = jnp.stack(window[2:]) - jnp.stack(window[:-2])
            dz = jnp.stack([ext[k + 2, row + i] - ext[k, row + i] for i in range(group)])
            before = jnp.where(lane == LANES - 1, pltpu.roll(center, 1, 1) * not_first, center)
            after = jnp.where(lane == 0, pltpu.roll(center, SUB - 1, 1) * not_last, center)
            dy = pltpu.roll(after, LANES - 1, 2) - pltpu.roll(before, 1, 2)
            square = dx * dx + dy * dy + dz * dz
            lambert = (0.48 * dx + 0.6 * dy + 0.64 * dz) * lax.rsqrt(jnp.maximum(square, 4.0))
            center_sq = center * center
            opacity = 1.0 - jnp.exp(-absorb * center_sq * center_sq)
            halved = opacity * (0.1 + 0.4 * jnp.abs(lambert))
            tilt = halved * jnp.tanh(center)
            green = halved + halved * jnp.tanh(0.5 - 0.5 * center_sq)
            for ch, value in enumerate((halved + tilt, green, halved - tilt, opacity)):
                edge = jnp.where(low_lanes, pltpu.roll(value, SUB - 1, 1), pltpu.roll(value, 1, 1)) * edge_mask
                place = pl.ds((ch * block + g * group) * SUB, rows)
                lhs[place, 0:LANES] = value.reshape(rows, LANES).astype(jnp.bfloat16)
                lhs[place, LANES : 2 * LANES] = edge.reshape(rows, LANES).astype(jnp.bfloat16)

    def resample(k, x0, lhs):
        value = jnp.dot(lhs[...], weights[...], preferred_element_type=jnp.float32)
        res[k, :, pl.ds(x0, block)] = value.reshape(4, block, SUB, LANES)

    def run(count, place):
        shade(*place(0), lhs0)

        def pair(i, last):
            resample(*place(2 * i), lhs0)
            shade(*place(2 * i + 1), lhs1)
            resample(*place(2 * i + 1), lhs1)
            if not last:
                shade(*place(2 * i + 2), lhs0)

        def body(i, carry):
            pair(i, False)
            return carry

        lax.fori_loop(0, count // 2 - 1, body, 0)
        pair(count // 2 - 1, True)

    left_blocks = -(-LEFT // block)
    assert left_blocks % 2 == 1
    mid_count = pairs - left_blocks // 2 - 1
    rim_count = pairs - mid_count
    mid_start = left_blocks // 2 + side
    mid_slices = slices - 2
    early = 2

    def give_place(t, first, count):
        t = jnp.int32(t)
        slot = lax.rem(first + lax.rem(t, count), pairs)
        return 1 + t // count, (2 * slot + 1 - side) * block

    def keep_place(t, first):
        t = jnp.int32(t)
        return first + t // pairs, (2 * lax.rem(t, pairs) + side) * block

    run(mid_slices * mid_count, lambda t: give_place(t, mid_start, mid_count))

    pl.when(has_right)(to_right.wait_send)
    pl.when(has_left)(to_left.wait_send)

    @pl.when(has_left)
    def _():
        to_right.wait_recv()
        ext[1 : slices + 1, 0:LEFT] = lrecv[...]

    @pl.when(has_right)
    def _():
        to_left.wait_recv()
        ext[1 : slices + 1, LEFT + columns : LEFT + columns + 1] = rrecv[...]

    @pl.when(jnp.logical_not(has_left))
    def _():
        ext[:, 0:LEFT] = jnp.zeros((slices + 2, LEFT, SUB, LANES), jnp.float32)

    @pl.when(jnp.logical_not(has_right))
    def _():
        ext[:, LEFT + columns : LEFT + columns + 1] = jnp.zeros((slices + 2, 1, SUB, LANES), jnp.float32)

    run(mid_slices * rim_count, lambda t: give_place(t, mid_start + mid_count, rim_count))
    run(early * pairs, lambda t: keep_place(t, 1))

    def decode_slice(slot, plane):
        def body(i, carry):
            word = zrecv[slot, pl.ds(i * 8, 8)]
            ext[plane, pl.ds(LEFT + i * 8, 8)] = density_value(low_half(word))
            ext[plane, pl.ds(LEFT + half + i * 8, 8)] = density_value(high_half(word))
            return carry

        lax.fori_loop(0, half // 8, body, 0)

    for slot, plane in ((0, 0), (1, slices + 1)):
        @pl.when(z_in[slot])
        def _(slot=slot, plane=plane):
            z_copies[slot].wait_recv()
            decode_slice(slot, plane)

        @pl.when(z_in[slot] & has_left)
        def _(slot=slot, plane=plane):
            c_copies[slot].wait_recv()
            ext[plane, pl.ds(1, SMAX)] = density_value(high_half(crecv[slot]))

        @pl.when(jnp.logical_not(z_in[slot]))
        def _(plane=plane):
            ext[plane] = jnp.zeros(ext.shape[1:], jnp.float32)

    def finish_block(number):
        start = number * block
        shade(0, start, lhs0)
        resample(0, start, lhs0)
        shade(slices - 1, start, lhs1)
        resample(slices - 1, start, lhs1)

    def column_partial(x):
        flip = [flips[x + u] for u in range(lump)]
        colour = [None] * 3
        transmit = None
        for i in range(slices):
            depths = [i + flip[u] * (slices - 1 - 2 * i) for u in range(lump)]
            through = 1.0 - jnp.stack([res[depths[u], 3, x + u] for u in range(lump)])
            for ch in range(3):
                value = jnp.stack([res[depths[u], ch, x + u] for u in range(lump)])
                colour[ch] = value if i == 0 else colour[ch] + transmit * value
            transmit = through if i == 0 else transmit * through
        return colour, transmit

    def store_codes(ref, slot, x, colour, opacity):
        span = pl.ds(x, lump)
        ref[slot, 0, span] = pack(image_code(colour[0]), image_code(colour[1]))
        ref[slot, 1, span] = pack(image_code(colour[2]), image_code(opacity))

    def load_codes(first, second):
        colour = [image_value(low_half(first)), image_value(high_half(first)), image_value(low_half(second))]
        return colour, image_value(high_half(second))

    def y_copy(slot):
        return remote(ysend.at[slot], yrecv.at[slot], y_send.at[slot], y_recv.at[slot], col, depth + 1 - 2 * side)

    def i_copy(slot):
        return remote(isend.at[slot], irecv.at[rank], i_send.at[slot], i_recv.at[rank], col, 2 * slot + side)

    def give(i, carry):
        slot = lax.rem(rank + 1 + i, pairs)
        number = 2 * slot + 1 - side
        finish_block(number)

        def body(step, inner_carry):
            x = step * lump
            colour, transmit = column_partial(number * block + x)
            store_codes(ysend, slot, x, colour, 1.0 - transmit)
            return inner_carry

        lax.fori_loop(0, block // lump, body, 0)
        y_copy(slot).start()
        return carry

    lax.fori_loop(0, pairs, give, 0)
    run((mid_slices - early) * pairs, lambda t: keep_place(t, 1 + early))

    def keep(i, carry):
        slot = lax.rem(rank + 1 + i, pairs)
        number = 2 * slot + side
        finish_block(number)

        def body(step, inner_carry):
            x = step * lump
            colour, transmit = column_partial(number * block + x)
            for ch in range(3):
                kept[ch, pl.ds(x, lump)] = colour[ch]
            kept[3, pl.ds(x, lump)] = transmit
            return inner_carry

        lax.fori_loop(0, block // lump, body, 0)
        y_copy(slot).wait_recv()

        def join(step, inner_carry):
            x = step * lump
            span = pl.ds(x, lump)
            theirs, their_opacity = load_codes(yrecv[slot, 0, span], yrecv[slot, 1, span])
            their_transmit = 1.0 - their_opacity
            mine = [kept[ch, span] for ch in range(3)]
            my_transmit = kept[3, span]
            flip = [jnp.full((SUB, LANES), flips[number * block + x + u], jnp.int32) for u in range(lump)]
            mine_first = jnp.stack(flip) == side
            front_transmit = jnp.where(mine_first, my_transmit, their_transmit)
            colour = []
            for ch in range(3):
                front = jnp.where(mine_first, mine[ch], theirs[ch])
                behind = jnp.where(mine_first, theirs[ch], mine[ch])
                colour.append(front + front_transmit * behind)
            opacity = 1.0 - my_transmit * their_transmit

            @pl.when(i < pairs - 1)
            def _():
                store_codes(isend, slot, x, colour, opacity)

            @pl.when(i == pairs - 1)
            def _():
                store_codes(irecv, rank, x, colour, opacity)

            return inner_carry

        lax.fori_loop(0, block // lump, join, 0)
        pl.when(i < pairs - 1)(lambda: i_copy(slot).start())
        return carry

    lax.fori_loop(0, pairs, keep, 0)

    def arrive(i, carry):
        slot = lax.rem(rank + i, pairs)
        remote(
            isend.at[slot], irecv.at[slot], i_send.at[slot], i_recv.at[slot], col, 2 * slot + side
        ).wait_recv()
        return carry

    lax.fori_loop(1, pairs, arrive, 0)

    def compose(step, carry):
        x = step * lump
        flip = [flips[depth * block + x + u] for u in range(lump)]
        colour = [None] * 3
        transmit = None
        for i in range(pairs):
            slot = [i + flip[u] * (pairs - 1 - 2 * i) for u in range(lump)]
            words = [jnp.stack([irecv[slot[u], part, x + u] for u in range(lump)]) for part in range(2)]
            value, opacity = load_codes(*words)
            for ch in range(3):
                colour[ch] = value[ch] if i == 0 else colour[ch] + transmit * value[ch]
            transmit = 1.0 - opacity if i == 0 else transmit * (1.0 - opacity)
        for ch in range(3):
            final[ch, pl.ds(x, lump)] = colour[ch]
        final[3, pl.ds(x, lump)] = 1.0 - transmit
        return carry

    lax.fori_loop(0, block // lump, compose, 0)
    part = min(8, block)
    for ch in range(4):
        for x0 in range(0, block, part):
            out[ch, x0 : x0 + part, :] = final[ch, x0 : x0 + part].reshape(part, height)

    for slot in range(2):
        pl.when(z_out[slot])(z_copies[slot].wait_send)
        pl.when(z_out[slot] & has_right)(c_copies[slot].wait_send)

    def left_y(i, carry):
        y_copy(i).wait_send()
        return carry

    lax.fori_loop(0, pairs, left_y, 0)

    def left_i(i, carry):
        i_copy(lax.rem(rank + i, pairs)).wait_send()
        return carry

    lax.fori_loop(1, pairs, left_i, 0)


def on_device(density, offsets, view_flip):
    col_count, depth_count = lax.axis_size("col"), lax.axis_size("depth")
    slices, columns, height = density.shape
    block = columns // depth_count
    pairs = depth_count // 2
    half = columns // 2
    f32, i32 = jnp.float32, jnp.int32
    dma = pltpu.SemaphoreType.DMA
    image = pltpu.VMEM((pairs, 2, block, SUB, LANES), i32)
    scratch = [
        pltpu.SMEM((slices,), i32),
        pltpu.SMEM((columns,), i32),
        pltpu.VMEM((2 * LANES, LANES), jnp.bfloat16),
        pltpu.VMEM((slices + 2, LEFT + columns + 1, SUB, LANES), f32),
        pltpu.VMEM((slices, LEFT, SUB, LANES), f32),
        pltpu.VMEM((slices, 1, SUB, LANES), f32),
        pltpu.VMEM((2, half, SUB, LANES), i32),
        pltpu.VMEM((2, half, SUB, LANES), i32),
        pltpu.VMEM((2, SMAX, SUB, LANES), i32),
        pltpu.VMEM((4 * block * SUB, 2 * LANES), jnp.bfloat16),
        pltpu.VMEM((4 * block * SUB, 2 * LANES), jnp.bfloat16),
        pltpu.VMEM((slices, 4, columns, SUB, LANES), f32),
        pltpu.VMEM((4, block, SUB, LANES), f32),
        image, image, image, image,
        pltpu.VMEM((4, block, SUB, LANES), f32),
        dma((2,)),
        dma((slices, SUB)),
        dma((2,)), dma((2,)), dma((2,)), dma((2,)), dma((2,)), dma((2,)),
        dma((pairs,)), dma((pairs,)), dma((pairs,)), dma((pairs,)),
    ]
    vmem = pl.BlockSpec(memory_space=pltpu.VMEM)
    hbm = pl.BlockSpec(memory_space=pltpu.HBM)
    return pl.pallas_call(
        functools.partial(kernel, col_count, depth_count),
        out_shape=jax.ShapeDtypeStruct((4, block, height), f32),
        in_specs=[hbm, hbm, hbm],
        out_specs=vmem,
        scratch_shapes=scratch,
        compiler_params=pltpu.CompilerParams(
            collective_id=0, has_side_effects=True, vmem_limit_bytes=63 * 2**20
        ),
    )(density, offsets, view_flip)


def solution(mesh):
    in_specs = (P("depth", "col", None), P("depth"), P("col"))
    out_specs = P(None, ("col", "depth"), None)
    return jax.shard_map(
        on_device, mesh=mesh, in_specs=in_specs, out_specs=out_specs, check_vma=False
    )
```

```python
import functools

import jax
import jax.numpy as jnp
from jax import lax
from jax.experimental import pallas as pl
from jax.experimental.pallas import tpu as pltpu
from jax.sharding import PartitionSpec as P

SMAX = 8
LEFT = SMAX + 1
SUB = 8
LANES = 128
MESH = pl.DeviceIdType.MESH
DENSITY_SCALE = 65535.0 / 12.0
IMAGE_SCALE = 65530.0


def pack(low, high):
    return low | lax.shift_left(high, jnp.full_like(high, 16))


def low_half(word):
    return (word & 0xFFFF).astype(jnp.float32)


def high_half(word):
    return lax.shift_right_logical(word, jnp.full_like(word, 16)).astype(jnp.float32)


def density_code(value):
    return ((value + 6.0) * DENSITY_SCALE + 0.5).astype(jnp.int32)


def density_value(code):
    return code * (1.0 / DENSITY_SCALE) - 6.0


def image_code(value):
    root = jnp.sqrt(jnp.sqrt(jnp.sqrt(value)))
    return (root * IMAGE_SCALE + 0.5).astype(jnp.int32)


def image_value(code):
    root = code * (1.0 / IMAGE_SCALE)
    square = root * root
    fourth = square * square
    return fourth * fourth


def kernel(
    col_count, depth_count,
    dens, offsets_in, flips_in, out,
    offsets, flips, weights, nat, ext, lrecv, rrecv, zsend, zrecv, crecv, lhs0, lhs1, res, kept,
    ysend, yrecv, isend, irecv, final, small_sem, in_sem, col_send, col_recv, z_send, z_recv, c_send, c_recv, y_send, y_recv, i_send, i_recv,
):
    slices, columns, height = dens.shape
    absorb = 0.5 / (slices * depth_count)
    block = columns // depth_count
    pairs = depth_count // 2
    half = columns // 2
    group = min(4, block)
    lump = min(4, block)
    col = lax.axis_index("col")
    depth = lax.axis_index("depth")
    side = lax.rem(depth, 2)
    rank = depth // 2
    has_left, has_right = col > 0, col < col_count - 1
    has_up, has_down = depth > 0, depth < depth_count - 1

    def at(c, d):
        return {"col": c, "depth": d}

    loads = [pltpu.make_async_copy(dens.at[k], nat.at[k], in_sem.at[k]) for k in range(slices)]
    for k in [0, slices - 1] + list(range(1, slices - 1)):
        loads[k].start()

    small = [
        pltpu.make_async_copy(offsets_in, offsets, small_sem.at[0]),
        pltpu.make_async_copy(flips_in, flips, small_sem.at[1]),
    ]
    for copy in small:
        copy.start()

    barrier = pltpu.get_barrier_semaphore()

    def greet(c, d):
        pl.semaphore_signal(barrier, inc=1, device_id=at(c, d), device_id_type=MESH)

    def greet_rank(i, carry):
        greet(col, lax.rem(rank + i, pairs) * 2 + side)
        return carry

    lax.fori_loop(1, pairs, greet_rank, 0)
    pl.when(has_up)(lambda: greet(col, depth - 1))
    pl.when(has_down)(lambda: greet(col, depth + 1))
    one = jnp.int32(1)
    none = jnp.int32(0)
    depth_sides = jnp.where(has_up, one, none) + jnp.where(has_down, one, none)
    col_sides = jnp.where(has_left, one, none) + jnp.where(has_right, one, none)
    for step, present in ((-1, has_left), (1, has_right)):
        pl.when(present)(lambda step=step: greet(col + step, depth))
        pl.when(present & has_up)(lambda step=step: greet(col + step, depth - 1))
        pl.when(present & has_down)(lambda step=step: greet(col + step, depth + 1))

    def move(k, x0):
        ext[k + 1, pl.ds(LEFT + x0, 8)] = nat[k, pl.ds(x0, 8), :].reshape(8, SUB, LANES)

    def relayout(k):
        def body(i, carry):
            for u in range(4):
                move(k, pl.multiple_of(i * 32 + u * 8, 8))
            return carry

        lax.fori_loop(0, columns // 32, body, 0)

    def encode_slice(slot, k):
        def body(i, carry):
            low = ext[k + 1, pl.ds(LEFT + i * 8, 8)]
            high = ext[k + 1, pl.ds(LEFT + half + i * 8, 8)]
            zsend[slot, pl.ds(i * 8, 8)] = pack(density_code(low), density_code(high))
            return carry

        lax.fori_loop(0, half // 8, body, 0)

    for k in (0, slices - 1):
        loads[k].wait()
        relayout(k)
    encode_slice(0, slices - 1)
    encode_slice(1, 0)
    pl.semaphore_wait(barrier, pairs - 1 + depth_sides + col_sides + col_sides * depth_sides)

    def remote(src, dst, send, recv, c, d):
        return pltpu.make_async_remote_copy(
            src_ref=src, dst_ref=dst, send_sem=send, recv_sem=recv, device_id=at(c, d), device_id_type=MESH
        )

    tail = pl.ds(half - SMAX, SMAX)
    z_copies = [
        remote(zsend.at[0], zrecv.at[0], z_send.at[0], z_recv.at[0], col, depth + 1),
        remote(zsend.at[1], zrecv.at[1], z_send.at[1], z_recv.at[1], col, depth - 1),
    ]
    c_copies = [
        remote(zsend.at[0, tail], crecv.at[0], c_send.at[0], c_recv.at[0], col + 1, depth + 1),
        remote(zsend.at[1, tail], crecv.at[1], c_send.at[1], c_recv.at[1], col + 1, depth - 1),
    ]
    z_out = (has_down, has_up)
    z_in = (has_up, has_down)
    for slot in range(2):
        pl.when(z_out[slot])(z_copies[slot].start)
        pl.when(z_out[slot] & has_right)(c_copies[slot].start)

    for k in range(1, slices - 1):
        loads[k].wait()
        for x0 in (0, columns - 16, columns - 8):
            move(k, x0)
    inner = pl.ds(1, slices)
    to_right = remote(ext.at[inner, pl.ds(columns, LEFT)], lrecv, col_send.at[0], col_recv.at[0], col + 1, depth)
    to_left = remote(ext.at[inner, pl.ds(LEFT, 1)], rrecv, col_send.at[1], col_recv.at[1], col - 1, depth)
    pl.when(has_right)(to_right.start)
    pl.when(has_left)(to_left.start)

    def relayout_inner(k, carry):
        def body(i, inner_carry):
            for u in range(4):
                move(k, pl.multiple_of(8 + jnp.minimum(i * 32 + u * 8, columns - 32), 8))
            return inner_carry

        return lax.fori_loop(0, columns // 32, body, carry)

    lax.fori_loop(1, slices - 1, relayout_inner, 0)

    source = lax.broadcasted_iota(jnp.int32, (LANES, LANES), 0)
    target = lax.broadcasted_iota(jnp.int32, (LANES, LANES), 1)

    def taps(distance):
        distance = jnp.abs(distance)
        return jnp.where(distance == 0, 0.5, jnp.where(distance == 1, 0.1875, jnp.where(distance == 2, 0.0625, 0.0)))

    weights[0:LANES, :] = taps(source - target).astype(jnp.bfloat16)
    shift = jnp.where(source < LANES // 2, LANES, -LANES)
    weights[LANES : 2 * LANES, :] = taps(source + shift - target).astype(jnp.bfloat16)
    for copy in small:
        copy.wait()

    shape = (group, SUB, LANES)
    lane = lax.broadcasted_iota(jnp.int32, shape, 2)
    sub = lax.broadcasted_iota(jnp.int32, shape, 1)
    not_first = jnp.where(sub == 0, 0.0, 1.0)
    not_last = jnp.where(sub == SUB - 1, 0.0, 1.0)
    low_lanes = lane < LANES // 2
    edge_mask = jnp.where(low_lanes, not_last, not_first)

    def shade(k, x0, lhs):
        for g in range(block // group):
            row = LEFT + x0 + g * group - offsets[k]
            rows = group * SUB
            window = [ext[k + 1, row + i] for i in range(-1, group + 1)]
            center = jnp.stack(window[1:-1])
            dx = jnp.stack(window[2:]) - jnp.stack(window[:-2])
            dz = jnp.stack([ext[k + 2, row + i] - ext[k, row + i] for i in range(group)])
            before = jnp.where(lane == LANES - 1, pltpu.roll(center, 1, 1) * not_first, center)
            after = jnp.where(lane == 0, pltpu.roll(center, SUB - 1, 1) * not_last, center)
            dy = pltpu.roll(after, LANES - 1, 2) - pltpu.roll(before, 1, 2)
            square = dx * dx + dy * dy + dz * dz
            lambert = (0.48 * dx + 0.6 * dy + 0.64 * dz) * lax.rsqrt(jnp.maximum(square, 4.0))
            center_sq = center * center
            opacity = 1.0 - jnp.exp(-absorb * center_sq * center_sq)
            halved = opacity * (0.1 + 0.4 * jnp.abs(lambert))
            tilt = halved * jnp.tanh(center)
            green = halved + halved * jnp.tanh(0.5 - 0.5 * center_sq)
            for ch, value in enumerate((halved + tilt, green, halved - tilt, opacity)):
                edge = jnp.where(low_lanes, pltpu.roll(value, SUB - 1, 1), pltpu.roll(value, 1, 1)) * edge_mask
                place = pl.ds((ch * block + g * group) * SUB, rows)
                lhs[place, 0:LANES] = value.reshape(rows, LANES).astype(jnp.bfloat16)
                lhs[place, LANES : 2 * LANES] = edge.reshape(rows, LANES).astype(jnp.bfloat16)

    def resample(k, x0, lhs):
        value = jnp.dot(lhs[...], weights[...], preferred_element_type=jnp.float32)
        res[k, :, pl.ds(x0, block)] = value.reshape(4, block, SUB, LANES)

    def run(count, place):
        shade(*place(0), lhs0)

        def pair(i, last):
            resample(*place(2 * i), lhs0)
            shade(*place(2 * i + 1), lhs1)
            resample(*place(2 * i + 1), lhs1)
            if not last:
                shade(*place(2 * i + 2), lhs0)

        def body(i, carry):
            pair(i, False)
            return carry

        lax.fori_loop(0, count // 2 - 1, body, 0)
        pair(count // 2 - 1, True)

    left_blocks = -(-LEFT // block)
    assert left_blocks % 2 == 1
    mid_count = pairs - left_blocks // 2 - 1
    rim_count = pairs - mid_count
    mid_start = left_blocks // 2 + side
    mid_slices = slices - 2
    early = 2

    def give_place(t, first, count):
        t = jnp.int32(t)
        slot = lax.rem(first + lax.rem(t, count), pairs)
        return 1 + t // count, (2 * slot + 1 - side) * block

    def keep_place(t, first):
        t = jnp.int32(t)
        return first + t // pairs, (2 * lax.rem(t, pairs) + side) * block

    run(mid_slices * mid_count, lambda t: give_place(t, mid_start, mid_count))

    pl.when(has_right)(to_right.wait_send)
    pl.when(has_left)(to_left.wait_send)

    @pl.when(has_left)
    def _():
        to_right.wait_recv()
        ext[1 : slices + 1, 0:LEFT] = lrecv[...]

    @pl.when(has_right)
    def _():
        to_left.wait_recv()
        ext[1 : slices + 1, LEFT + columns : LEFT + columns + 1] = rrecv[...]

    @pl.when(jnp.logical_not(has_left))
    def _():
        ext[:, 0:LEFT] = jnp.zeros((slices + 2, LEFT, SUB, LANES), jnp.float32)

    @pl.when(jnp.logical_not(has_right))
    def _():
        ext[:, LEFT + columns : LEFT + columns + 1] = jnp.zeros((slices + 2, 1, SUB, LANES), jnp.float32)

    run(mid_slices * rim_count, lambda t: give_place(t, mid_start + mid_count, rim_count))
    run(early * pairs, lambda t: keep_place(t, 1))

    def decode_slice(slot, plane):
        def body(i, carry):
            word = zrecv[slot, pl.ds(i * 8, 8)]
            ext[plane, pl.ds(LEFT + i * 8, 8)] = density_value(low_half(word))
            ext[plane, pl.ds(LEFT + half + i * 8, 8)] = density_value(high_half(word))
            return carry

        lax.fori_loop(0, half // 8, body, 0)

    for slot, plane in ((0, 0), (1, slices + 1)):
        @pl.when(z_in[slot])
        def _(slot=slot, plane=plane):
            z_copies[slot].wait_recv()
            decode_slice(slot, plane)

        @pl.when(z_in[slot] & has_left)
        def _(slot=slot, plane=plane):
            c_copies[slot].wait_recv()
            ext[plane, pl.ds(1, SMAX)] = density_value(high_half(crecv[slot]))

        @pl.when(jnp.logical_not(z_in[slot]))
        def _(plane=plane):
            ext[plane] = jnp.zeros(ext.shape[1:], jnp.float32)

    def finish_block(number):
        start = number * block
        shade(0, start, lhs0)
        resample(0, start, lhs0)
        shade(slices - 1, start, lhs1)
        resample(slices - 1, start, lhs1)

    def column_partial(x):
        flip = [flips[x + u] for u in range(lump)]
        colour = [None] * 3
        transmit = None
        for i in range(slices):
            depths = [i + flip[u] * (slices - 1 - 2 * i) for u in range(lump)]
            through = 1.0 - jnp.stack([res[depths[u], 3, x + u] for u in range(lump)])
            for ch in range(3):
                value = jnp.stack([res[depths[u], ch, x + u] for u in range(lump)])
                colour[ch] = value if i == 0 else colour[ch] + transmit * value
            transmit = through if i == 0 else transmit * through
        return colour, transmit

    def store_codes(ref, slot, x, colour, opacity):
        span = pl.ds(x, lump)
        ref[slot, 0, span] = pack(image_code(colour[0]), image_code(colour[1]))
        ref[slot, 1, span] = pack(image_code(colour[2]), image_code(opacity))

    def load_codes(first, second):
        colour = [image_value(low_half(first)), image_value(high_half(first)), image_value(low_half(second))]
        return colour, image_value(high_half(second))

    def y_copy(slot):
        return remote(ysend.at[slot], yrecv.at[slot], y_send.at[slot], y_recv.at[slot], col, depth + 1 - 2 * side)

    def i_copy(slot):
        return remote(isend.at[slot], irecv.at[rank], i_send.at[slot], i_recv.at[rank], col, 2 * slot + side)

    def give(i, carry):
        slot = lax.rem(rank + 1 + i, pairs)
        number = 2 * slot + 1 - side
        finish_block(number)

        def body(step, inner_carry):
            x = step * lump
            colour, transmit = column_partial(number * block + x)
            store_codes(ysend, slot, x, colour, 1.0 - transmit)
            return inner_carry

        lax.fori_loop(0, block // lump, body, 0)
        y_copy(slot).start()
        return carry

    lax.fori_loop(0, pairs, give, 0)
    run((mid_slices - early) * pairs, lambda t: keep_place(t, 1 + early))

    def keep(i, carry):
        slot = lax.rem(rank + 1 + i, pairs)
        number = 2 * slot + side
        finish_block(number)

        def body(step, inner_carry):
            x = step * lump
            colour, transmit = column_partial(number * block + x)
            for ch in range(3):
                kept[ch, pl.ds(x, lump)] = colour[ch]
            kept[3, pl.ds(x, lump)] = transmit
            return inner_carry

        lax.fori_loop(0, block // lump, body, 0)
        y_copy(slot).wait_recv()

        def join(step, inner_carry):
            x = step * lump
            span = pl.ds(x, lump)
            theirs, their_opacity = load_codes(yrecv[slot, 0, span], yrecv[slot, 1, span])
            their_transmit = 1.0 - their_opacity
            mine = [kept[ch, span] for ch in range(3)]
            my_transmit = kept[3, span]
            flip = [jnp.full((SUB, LANES), flips[number * block + x + u], jnp.int32) for u in range(lump)]
            mine_first = jnp.stack(flip) == side
            front_transmit = jnp.where(mine_first, my_transmit, their_transmit)
            colour = []
            for ch in range(3):
                front = jnp.where(mine_first, mine[ch], theirs[ch])
                behind = jnp.where(mine_first, theirs[ch], mine[ch])
                colour.append(front + front_transmit * behind)
            opacity = 1.0 - my_transmit * their_transmit

            @pl.when(i < pairs - 1)
            def _():
                store_codes(isend, slot, x, colour, opacity)

            @pl.when(i == pairs - 1)
            def _():
                store_codes(irecv, rank, x, colour, opacity)

            return inner_carry

        lax.fori_loop(0, block // lump, join, 0)
        pl.when(i < pairs - 1)(lambda: i_copy(slot).start())
        return carry

    lax.fori_loop(0, pairs, keep, 0)

    def arrive(i, carry):
        slot = lax.rem(rank + i, pairs)
        remote(
            isend.at[slot], irecv.at[slot], i_send.at[slot], i_recv.at[slot], col, 2 * slot + side
        ).wait_recv()
        return carry

    lax.fori_loop(1, pairs, arrive, 0)

    def compose(step, carry):
        x = step * lump
        flip = [flips[depth * block + x + u] for u in range(lump)]
        colour = [None] * 3
        transmit = None
        for i in range(pairs):
            slot = [i + flip[u] * (pairs - 1 - 2 * i) for u in range(lump)]
            words = [jnp.stack([irecv[slot[u], part, x + u] for u in range(lump)]) for part in range(2)]
            value, opacity = load_codes(*words)
            for ch in range(3):
                colour[ch] = value[ch] if i == 0 else colour[ch] + transmit * value[ch]
            transmit = 1.0 - opacity if i == 0 else transmit * (1.0 - opacity)
        for ch in range(3):
            final[ch, pl.ds(x, lump)] = colour[ch]
        final[3, pl.ds(x, lump)] = 1.0 - transmit
        return carry

    lax.fori_loop(0, block // lump, compose, 0)
    part = min(8, block)
    for ch in range(4):
        for x0 in range(0, block, part):
            out[ch, x0 : x0 + part, :] = final[ch, x0 : x0 + part].reshape(part, height)

    for slot in range(2):
        pl.when(z_out[slot])(z_copies[slot].wait_send)
        pl.when(z_out[slot] & has_right)(c_copies[slot].wait_send)

    def left_y(i, carry):
        y_copy(i).wait_send()
        return carry

    lax.fori_loop(0, pairs, left_y, 0)

    def left_i(i, carry):
        i_copy(lax.rem(rank + i, pairs)).wait_send()
        return carry

    lax.fori_loop(1, pairs, left_i, 0)


def on_device(density, offsets, view_flip):
    col_count, depth_count = lax.axis_size("col"), lax.axis_size("depth")
    slices, columns, height = density.shape
    block = columns // depth_count
    pairs = depth_count // 2
    half = columns // 2
    f32, i32 = jnp.float32, jnp.int32
    dma = pltpu.SemaphoreType.DMA
    image = pltpu.VMEM((pairs, 2, block, SUB, LANES), i32)
    scratch = [
        pltpu.SMEM((slices,), i32),
        pltpu.SMEM((columns,), i32),
        pltpu.VMEM((2 * LANES, LANES), jnp.bfloat16),
        pltpu.VMEM((slices, columns, height), f32),
        pltpu.VMEM((slices + 2, LEFT + columns + 1, SUB, LANES), f32),
        pltpu.VMEM((slices, LEFT, SUB, LANES), f32),
        pltpu.VMEM((slices, 1, SUB, LANES), f32),
        pltpu.VMEM((2, half, SUB, LANES), i32),
        pltpu.VMEM((2, half, SUB, LANES), i32),
        pltpu.VMEM((2, SMAX, SUB, LANES), i32),
        pltpu.VMEM((4 * block * SUB, 2 * LANES), jnp.bfloat16),
        pltpu.VMEM((4 * block * SUB, 2 * LANES), jnp.bfloat16),
        pltpu.VMEM((slices, 4, columns, SUB, LANES), f32),
        pltpu.VMEM((4, block, SUB, LANES), f32),
        image, image, image, image,
        pltpu.VMEM((4, block, SUB, LANES), f32),
        dma((2,)),
        dma((slices,)),
        dma((2,)), dma((2,)), dma((2,)), dma((2,)), dma((2,)), dma((2,)),
        dma((pairs,)), dma((pairs,)), dma((pairs,)), dma((pairs,)),
    ]
    vmem = pl.BlockSpec(memory_space=pltpu.VMEM)
    hbm = pl.BlockSpec(memory_space=pltpu.HBM)
    return pl.pallas_call(
        functools.partial(kernel, col_count, depth_count),
        out_shape=jax.ShapeDtypeStruct((4, block, height), f32),
        in_specs=[hbm, hbm, hbm],
        out_specs=vmem,
        scratch_shapes=scratch,
        compiler_params=pltpu.CompilerParams(
            collective_id=0, has_side_effects=True, vmem_limit_bytes=63 * 2**20
        ),
    )(density, offsets, view_flip)


def solution(mesh):
    in_specs = (P("depth", "col", None), P("depth"), P("col"))
    out_specs = P(None, ("col", "depth"), None)
    return jax.shard_map(
        on_device, mesh=mesh, in_specs=in_specs, out_specs=out_specs, check_vma=False
    )
```

```python
import functools

import jax
import jax.numpy as jnp
from jax import lax
from jax.experimental import pallas as pl
from jax.experimental.pallas import tpu as pltpu
from jax.sharding import PartitionSpec as P

SMAX = 8
LEFT = SMAX + 1
SUB = 8
LANES = 128
MESH = pl.DeviceIdType.MESH
DENSITY_SCALE = 65535.0 / 12.0
IMAGE_SCALE = 65530.0


def pack(low, high):
    return low | lax.shift_left(high, jnp.full_like(high, 16))


def low_half(word):
    return (word & 0xFFFF).astype(jnp.float32)


def high_half(word):
    return lax.shift_right_logical(word, jnp.full_like(word, 16)).astype(jnp.float32)


def density_code(value):
    return ((value + 6.0) * DENSITY_SCALE + 0.5).astype(jnp.int32)


def density_value(code):
    return code * (1.0 / DENSITY_SCALE) - 6.0


def image_code(value):
    root = jnp.sqrt(jnp.sqrt(jnp.sqrt(value)))
    return (root * IMAGE_SCALE + 0.5).astype(jnp.int32)


def image_value(code):
    root = code * (1.0 / IMAGE_SCALE)
    square = root * root
    fourth = square * square
    return fourth * fourth


def kernel(
    col_count, depth_count,
    dens, offsets_in, flips_in, out,
    offsets, flips, weights, nat, ext, lrecv, rrecv, zsend, zrecv, crecv, lhs0, lhs1, res, kept,
    ysend, yrecv, isend, irecv, final, small_sem, in_sem, col_send, col_recv, z_send, z_recv, c_send, c_recv, y_send, y_recv, i_send, i_recv,
):
    slices, columns, height = dens.shape
    absorb = 0.5 / (slices * depth_count)
    block = columns // depth_count
    pairs = depth_count // 2
    half = columns // 2
    group = min(2, block)
    lump = min(4, block)
    col = lax.axis_index("col")
    depth = lax.axis_index("depth")
    side = lax.rem(depth, 2)
    rank = depth // 2
    has_left, has_right = col > 0, col < col_count - 1
    has_up, has_down = depth > 0, depth < depth_count - 1

    def at(c, d):
        return {"col": c, "depth": d}

    loads = [pltpu.make_async_copy(dens.at[k], nat.at[k], in_sem.at[k]) for k in range(slices)]
    for k in [0, slices - 1] + list(range(1, slices - 1)):
        loads[k].start()

    small = [
        pltpu.make_async_copy(offsets_in, offsets, small_sem.at[0]),
        pltpu.make_async_copy(flips_in, flips, small_sem.at[1]),
    ]
    for copy in small:
        copy.start()

    barrier = pltpu.get_barrier_semaphore()

    def greet(c, d):
        pl.semaphore_signal(barrier, inc=1, device_id=at(c, d), device_id_type=MESH)

    def greet_rank(i, carry):
        greet(col, lax.rem(rank + i, pairs) * 2 + side)
        return carry

    lax.fori_loop(1, pairs, greet_rank, 0)
    pl.when(has_up)(lambda: greet(col, depth - 1))
    pl.when(has_down)(lambda: greet(col, depth + 1))
    one = jnp.int32(1)
    none = jnp.int32(0)
    depth_sides = jnp.where(has_up, one, none) + jnp.where(has_down, one, none)
    col_sides = jnp.where(has_left, one, none) + jnp.where(has_right, one, none)
    for step, present in ((-1, has_left), (1, has_right)):
        pl.when(present)(lambda step=step: greet(col + step, depth))
        pl.when(present & has_up)(lambda step=step: greet(col + step, depth - 1))
        pl.when(present & has_down)(lambda step=step: greet(col + step, depth + 1))

    def move(k, x0):
        ext[k + 1, pl.ds(LEFT + x0, 8)] = nat[k, pl.ds(x0, 8), :].reshape(8, SUB, LANES)

    def relayout(k):
        def body(i, carry):
            for u in range(4):
                move(k, pl.multiple_of(i * 32 + u * 8, 8))
            return carry

        lax.fori_loop(0, columns // 32, body, 0)

    def encode_slice(slot, k):
        def body(i, carry):
            low = ext[k + 1, pl.ds(LEFT + i * 8, 8)]
            high = ext[k + 1, pl.ds(LEFT + half + i * 8, 8)]
            zsend[slot, pl.ds(i * 8, 8)] = pack(density_code(low), density_code(high))
            return carry

        lax.fori_loop(0, half // 8, body, 0)

    for k in (0, slices - 1):
        loads[k].wait()
        relayout(k)
    encode_slice(0, slices - 1)
    encode_slice(1, 0)
    pl.semaphore_wait(barrier, pairs - 1 + depth_sides + col_sides + col_sides * depth_sides)

    def remote(src, dst, send, recv, c, d):
        return pltpu.make_async_remote_copy(
            src_ref=src, dst_ref=dst, send_sem=send, recv_sem=recv, device_id=at(c, d), device_id_type=MESH
        )

    tail = pl.ds(half - SMAX, SMAX)
    z_copies = [
        remote(zsend.at[0], zrecv.at[0], z_send.at[0], z_recv.at[0], col, depth + 1),
        remote(zsend.at[1], zrecv.at[1], z_send.at[1], z_recv.at[1], col, depth - 1),
    ]
    c_copies = [
        remote(zsend.at[0, tail], crecv.at[0], c_send.at[0], c_recv.at[0], col + 1, depth + 1),
        remote(zsend.at[1, tail], crecv.at[1], c_send.at[1], c_recv.at[1], col + 1, depth - 1),
    ]
    z_out = (has_down, has_up)
    z_in = (has_up, has_down)
    for slot in range(2):
        pl.when(z_out[slot])(z_copies[slot].start)
        pl.when(z_out[slot] & has_right)(c_copies[slot].start)

    for k in range(1, slices - 1):
        loads[k].wait()
        for x0 in (0, columns - 16, columns - 8):
            move(k, x0)
    inner = pl.ds(1, slices)
    to_right = remote(ext.at[inner, pl.ds(columns, LEFT)], lrecv, col_send.at[0], col_recv.at[0], col + 1, depth)
    to_left = remote(ext.at[inner, pl.ds(LEFT, 1)], rrecv, col_send.at[1], col_recv.at[1], col - 1, depth)
    pl.when(has_right)(to_right.start)
    pl.when(has_left)(to_left.start)

    def relayout_inner(k, carry):
        def body(i, inner_carry):
            for u in range(4):
                move(k, pl.multiple_of(8 + jnp.minimum(i * 32 + u * 8, columns - 32), 8))
            return inner_carry

        return lax.fori_loop(0, columns // 32, body, carry)

    lax.fori_loop(1, slices - 1, relayout_inner, 0)

    source = lax.broadcasted_iota(jnp.int32, (LANES, LANES), 0)
    target = lax.broadcasted_iota(jnp.int32, (LANES, LANES), 1)

    def taps(distance):
        distance = jnp.abs(distance)
        return jnp.where(distance == 0, 0.5, jnp.where(distance == 1, 0.1875, jnp.where(distance == 2, 0.0625, 0.0)))

    weights[0:LANES, :] = taps(source - target).astype(jnp.bfloat16)
    shift = jnp.where(source < LANES // 2, LANES, -LANES)
    weights[LANES : 2 * LANES, :] = taps(source + shift - target).astype(jnp.bfloat16)
    for copy in small:
        copy.wait()

    shape = (group, SUB, LANES)
    lane = lax.broadcasted_iota(jnp.int32, (SUB, LANES), 1)
    sub = lax.broadcasted_iota(jnp.int32, (SUB, LANES), 0)
    not_first = jnp.where(sub == 0, 0.0, 1.0)[None]
    not_last = jnp.where(sub == SUB - 1, 0.0, 1.0)[None]
    edge_mask = jnp.where(lane < LANES // 2, not_last[0], not_first[0])[None]

    def pick(mask, first, second):
        return jnp.where(jnp.broadcast_to(mask[None], first.shape), first, second)

    def shade(k, x0, lhs):
        for g in range(block // group):
            row = LEFT + x0 + g * group - offsets[k]
            rows = group * SUB
            window = [ext[k + 1, row + i] for i in range(-1, group + 1)]
            center = jnp.stack(window[1:-1])
            dx = jnp.stack(window[2:]) - jnp.stack(window[:-2])
            dz = jnp.stack([ext[k + 2, row + i] - ext[k, row + i] for i in range(group)])
            before = pick(lane == LANES - 1, pltpu.roll(center, 1, 1) * not_first, center)
            after = pick(lane == 0, pltpu.roll(center, SUB - 1, 1) * not_last, center)
            dy = pltpu.roll(after, LANES - 1, 2) - pltpu.roll(before, 1, 2)
            square = dx * dx + dy * dy + dz * dz
            lambert = (0.48 * dx + 0.6 * dy + 0.64 * dz) * lax.rsqrt(jnp.maximum(square, 4.0))
            center_sq = center * center
            opacity = 1.0 - jnp.exp(-absorb * center_sq * center_sq)
            halved = opacity * (0.1 + 0.4 * jnp.abs(lambert))
            tilt = halved * jnp.tanh(center)
            green = halved + halved * jnp.tanh(0.5 - 0.5 * center_sq)
            for ch, value in enumerate((halved + tilt, green, halved - tilt, opacity)):
                edge = pick(lane < LANES // 2, pltpu.roll(value, SUB - 1, 1), pltpu.roll(value, 1, 1)) * edge_mask
                place = pl.ds((ch * block + g * group) * SUB, rows)
                lhs[place, 0:LANES] = value.reshape(rows, LANES).astype(jnp.bfloat16)
                lhs[place, LANES : 2 * LANES] = edge.reshape(rows, LANES).astype(jnp.bfloat16)

    def resample(k, x0, lhs):
        value = jnp.dot(lhs[...], weights[...], preferred_element_type=jnp.float32)
        res[k, :, pl.ds(x0, block)] = value.reshape(4, block, SUB, LANES)

    def run(count, place):
        shade(*place(0), lhs0)

        def pair(i, last):
            resample(*place(2 * i), lhs0)
            shade(*place(2 * i + 1), lhs1)
            resample(*place(2 * i + 1), lhs1)
            if not last:
                shade(*place(2 * i + 2), lhs0)

        def body(i, carry):
            pair(i, False)
            return carry

        lax.fori_loop(0, count // 2 - 1, body, 0)
        pair(count // 2 - 1, True)

    left_blocks = -(-LEFT // block)
    assert left_blocks % 2 == 1
    mid_count = pairs - left_blocks // 2 - 1
    rim_count = pairs - mid_count
    mid_start = left_blocks // 2 + side
    mid_slices = slices - 2
    early = 2

    def give_place(t, first, count):
        t = jnp.int32(t)
        slot = lax.rem(first + lax.rem(t, count), pairs)
        return 1 + t // count, (2 * slot + 1 - side) * block

    def keep_place(t, first):
        t = jnp.int32(t)
        return first + t // pairs, (2 * lax.rem(t, pairs) + side) * block

    run(mid_slices * mid_count, lambda t: give_place(t, mid_start, mid_count))

    pl.when(has_right)(to_right.wait_send)
    pl.when(has_left)(to_left.wait_send)

    @pl.when(has_left)
    def _():
        to_right.wait_recv()
        ext[1 : slices + 1, 0:LEFT] = lrecv[...]

    @pl.when(has_right)
    def _():
        to_left.wait_recv()
        ext[1 : slices + 1, LEFT + columns : LEFT + columns + 1] = rrecv[...]

    @pl.when(jnp.logical_not(has_left))
    def _():
        ext[:, 0:LEFT] = jnp.zeros((slices + 2, LEFT, SUB, LANES), jnp.float32)

    @pl.when(jnp.logical_not(has_right))
    def _():
        ext[:, LEFT + columns : LEFT + columns + 1] = jnp.zeros((slices + 2, 1, SUB, LANES), jnp.float32)

    run(mid_slices * rim_count, lambda t: give_place(t, mid_start + mid_count, rim_count))
    run(early * pairs, lambda t: keep_place(t, 1))

    def decode_slice(slot, plane):
        def body(i, carry):
            word = zrecv[slot, pl.ds(i * 8, 8)]
            ext[plane, pl.ds(LEFT + i * 8, 8)] = density_value(low_half(word))
            ext[plane, pl.ds(LEFT + half + i * 8, 8)] = density_value(high_half(word))
            return carry

        lax.fori_loop(0, half // 8, body, 0)

    for slot, plane in ((0, 0), (1, slices + 1)):
        @pl.when(z_in[slot])
        def _(slot=slot, plane=plane):
            z_copies[slot].wait_recv()
            decode_slice(slot, plane)

        @pl.when(z_in[slot] & has_left)
        def _(slot=slot, plane=plane):
            c_copies[slot].wait_recv()
            ext[plane, pl.ds(1, SMAX)] = density_value(high_half(crecv[slot]))

        @pl.when(jnp.logical_not(z_in[slot]))
        def _(plane=plane):
            ext[plane] = jnp.zeros(ext.shape[1:], jnp.float32)

    def finish_block(number):
        start = number * block
        shade(0, start, lhs0)
        resample(0, start, lhs0)
        shade(slices - 1, start, lhs1)
        resample(slices - 1, start, lhs1)

    def column_partial(x):
        flip = [flips[x + u] for u in range(lump)]
        colour = [None] * 3
        transmit = None
        for i in range(slices):
            depths = [i + flip[u] * (slices - 1 - 2 * i) for u in range(lump)]
            through = 1.0 - jnp.stack([res[depths[u], 3, x + u] for u in range(lump)])
            for ch in range(3):
                value = jnp.stack([res[depths[u], ch, x + u] for u in range(lump)])
                colour[ch] = value if i == 0 else colour[ch] + transmit * value
            transmit = through if i == 0 else transmit * through
        return colour, transmit

    def store_codes(ref, slot, x, colour, opacity):
        span = pl.ds(x, lump)
        ref[slot, 0, span] = pack(image_code(colour[0]), image_code(colour[1]))
        ref[slot, 1, span] = pack(image_code(colour[2]), image_code(opacity))

    def load_codes(first, second):
        colour = [image_value(low_half(first)), image_value(high_half(first)), image_value(low_half(second))]
        return colour, image_value(high_half(second))

    def y_copy(slot):
        return remote(ysend.at[slot], yrecv.at[slot], y_send.at[slot], y_recv.at[slot], col, depth + 1 - 2 * side)

    def i_copy(slot):
        return remote(isend.at[slot], irecv.at[rank], i_send.at[slot], i_recv.at[rank], col, 2 * slot + side)

    def give(i, carry):
        slot = lax.rem(rank + 1 + i, pairs)
        number = 2 * slot + 1 - side
        finish_block(number)

        for x in range(0, block, lump):
            colour, transmit = column_partial(number * block + x)
            store_codes(ysend, slot, x, colour, 1.0 - transmit)
        y_copy(slot).start()
        return carry

    lax.fori_loop(0, pairs, give, 0)
    run((mid_slices - early) * pairs, lambda t: keep_place(t, 1 + early))

    def keep(i, carry):
        slot = lax.rem(rank + 1 + i, pairs)
        number = 2 * slot + side
        finish_block(number)

        for x in range(0, block, lump):
            colour, transmit = column_partial(number * block + x)
            for ch in range(3):
                kept[ch, pl.ds(x, lump)] = colour[ch]
            kept[3, pl.ds(x, lump)] = transmit
        y_copy(slot).wait_recv()

        for x in range(0, block, lump):
            span = pl.ds(x, lump)
            theirs, their_opacity = load_codes(yrecv[slot, 0, span], yrecv[slot, 1, span])
            their_transmit = 1.0 - their_opacity
            mine = [kept[ch, span] for ch in range(3)]
            my_transmit = kept[3, span]
            flip = [jnp.full((SUB, LANES), flips[number * block + x + u], jnp.int32) for u in range(lump)]
            mine_first = jnp.stack(flip) == side
            front_transmit = jnp.where(mine_first, my_transmit, their_transmit)
            colour = []
            for ch in range(3):
                front = jnp.where(mine_first, mine[ch], theirs[ch])
                behind = jnp.where(mine_first, theirs[ch], mine[ch])
                colour.append(front + front_transmit * behind)
            opacity = 1.0 - my_transmit * their_transmit

            store_codes(isend, slot, x, colour, opacity)
            store_codes(irecv, rank, x, colour, opacity)
        pl.when(i < pairs - 1)(lambda: i_copy(slot).start())
        return carry

    lax.fori_loop(0, pairs, keep, 0)

    def arrive(i, carry):
        slot = lax.rem(rank + i, pairs)
        remote(
            isend.at[slot], irecv.at[slot], i_send.at[slot], i_recv.at[slot], col, 2 * slot + side
        ).wait_recv()
        return carry

    lax.fori_loop(1, pairs, arrive, 0)

    for x in range(0, block, lump):
        flip = [flips[depth * block + x + u] for u in range(lump)]
        colour = [None] * 3
        transmit = None
        for i in range(pairs):
            slot = [i + flip[u] * (pairs - 1 - 2 * i) for u in range(lump)]
            words = [jnp.stack([irecv[slot[u], part, x + u] for u in range(lump)]) for part in range(2)]
            value, opacity = load_codes(*words)
            for ch in range(3):
                colour[ch] = value[ch] if i == 0 else colour[ch] + transmit * value[ch]
            transmit = 1.0 - opacity if i == 0 else transmit * (1.0 - opacity)
        for ch in range(3):
            final[ch, pl.ds(x, lump)] = colour[ch]
        final[3, pl.ds(x, lump)] = 1.0 - transmit
    part = min(8, block)
    for ch in range(4):
        for x0 in range(0, block, part):
            out[ch, x0 : x0 + part, :] = final[ch, x0 : x0 + part].reshape(part, height)

    for slot in range(2):
        pl.when(z_out[slot])(z_copies[slot].wait_send)
        pl.when(z_out[slot] & has_right)(c_copies[slot].wait_send)

    def left_y(i, carry):
        y_copy(i).wait_send()
        return carry

    lax.fori_loop(0, pairs, left_y, 0)

    def left_i(i, carry):
        i_copy(lax.rem(rank + i, pairs)).wait_send()
        return carry

    lax.fori_loop(1, pairs, left_i, 0)


def on_device(density, offsets, view_flip):
    col_count, depth_count = lax.axis_size("col"), lax.axis_size("depth")
    slices, columns, height = density.shape
    block = columns // depth_count
    pairs = depth_count // 2
    half = columns // 2
    f32, i32 = jnp.float32, jnp.int32
    dma = pltpu.SemaphoreType.DMA
    image = pltpu.VMEM((pairs, 2, block, SUB, LANES), i32)
    scratch = [
        pltpu.SMEM((slices,), i32),
        pltpu.SMEM((columns,), i32),
        pltpu.VMEM((2 * LANES, LANES), jnp.bfloat16),
        pltpu.VMEM((slices, columns, height), f32),
        pltpu.VMEM((slices + 2, LEFT + columns + 1, SUB, LANES), f32),
        pltpu.VMEM((slices, LEFT, SUB, LANES), f32),
        pltpu.VMEM((slices, 1, SUB, LANES), f32),
        pltpu.VMEM((2, half, SUB, LANES), i32),
        pltpu.VMEM((2, half, SUB, LANES), i32),
        pltpu.VMEM((2, SMAX, SUB, LANES), i32),
        pltpu.VMEM((4 * block * SUB, 2 * LANES), jnp.bfloat16),
        pltpu.VMEM((4 * block * SUB, 2 * LANES), jnp.bfloat16),
        pltpu.VMEM((slices, 4, columns, SUB, LANES), f32),
        pltpu.VMEM((4, block, SUB, LANES), f32),
        image, image, image, image,
        pltpu.VMEM((4, block, SUB, LANES), f32),
        dma((2,)),
        dma((slices,)),
        dma((2,)), dma((2,)), dma((2,)), dma((2,)), dma((2,)), dma((2,)),
        dma((pairs,)), dma((pairs,)), dma((pairs,)), dma((pairs,)),
    ]
    vmem = pl.BlockSpec(memory_space=pltpu.VMEM)
    hbm = pl.BlockSpec(memory_space=pltpu.HBM)
    return pl.pallas_call(
        functools.partial(kernel, col_count, depth_count),
        out_shape=jax.ShapeDtypeStruct((4, block, height), f32),
        in_specs=[hbm, hbm, hbm],
        out_specs=vmem,
        scratch_shapes=scratch,
        compiler_params=pltpu.CompilerParams(
            collective_id=0, has_side_effects=True, vmem_limit_bytes=63 * 2**20
        ),
    )(density, offsets, view_flip)


def solution(mesh):
    in_specs = (P("depth", "col", None), P("depth"), P("col"))
    out_specs = P(None, ("col", "depth"), None)
    return jax.shard_map(
        on_device, mesh=mesh, in_specs=in_specs, out_specs=out_specs, check_vma=False
    )
```

```python
import functools

import jax
import jax.numpy as jnp
from jax import lax
from jax.experimental import pallas as pl
from jax.experimental.pallas import tpu as pltpu
from jax.sharding import PartitionSpec as P

SMAX = 8
LEFT = SMAX + 1
SUB = 8
LANES = 128
MESH = pl.DeviceIdType.MESH
DENSITY_SCALE = 65535.0 / 12.0
IMAGE_SCALE = 65530.0


def pack(low, high):
    return low | lax.shift_left(high, jnp.full_like(high, 16))


def low_half(word):
    return (word & 0xFFFF).astype(jnp.float32)


def high_half(word):
    return lax.shift_right_logical(word, jnp.full_like(word, 16)).astype(jnp.float32)


def density_code(value):
    return ((value + 6.0) * DENSITY_SCALE + 0.5).astype(jnp.int32)


def density_value(code):
    return code * (1.0 / DENSITY_SCALE) - 6.0


def image_code(value):
    root = jnp.sqrt(jnp.sqrt(jnp.sqrt(value)))
    return (root * IMAGE_SCALE + 0.5).astype(jnp.int32)


def image_value(code):
    root = code * (1.0 / IMAGE_SCALE)
    square = root * root
    fourth = square * square
    return fourth * fourth


def kernel(
    col_count, depth_count,
    dens, offsets_in, flips_in, out,
    offsets, flips, weights, nat, ext, lrecv, rrecv, zsend, zrecv, crecv, lhs0, lhs1, res, kept,
    ysend, yrecv, isend, irecv, final, small_sem, in_sem, col_send, col_recv, z_send, z_recv, c_send, c_recv, y_send, y_recv, i_send, i_recv,
):
    slices, columns, height = dens.shape
    absorb = 0.5 / (slices * depth_count)
    block = columns // depth_count
    pairs = depth_count // 2
    half = columns // 2
    group = min(2, block)
    lump = min(4, block)
    col = lax.axis_index("col")
    depth = lax.axis_index("depth")
    side = lax.rem(depth, 2)
    rank = depth // 2
    has_left, has_right = col > 0, col < col_count - 1
    has_up, has_down = depth > 0, depth < depth_count - 1

    def at(c, d):
        return {"col": c, "depth": d}

    loads = [pltpu.make_async_copy(dens.at[k], nat.at[k], in_sem.at[k]) for k in range(slices)]
    for k in [0, slices - 1] + list(range(1, slices - 1)):
        loads[k].start()

    small = [
        pltpu.make_async_copy(offsets_in, offsets, small_sem.at[0]),
        pltpu.make_async_copy(flips_in, flips, small_sem.at[1]),
    ]
    for copy in small:
        copy.start()

    barrier = pltpu.get_barrier_semaphore()

    def greet(c, d):
        pl.semaphore_signal(barrier, inc=1, device_id=at(c, d), device_id_type=MESH)

    def greet_rank(i, carry):
        greet(col, lax.rem(rank + i, pairs) * 2 + side)
        return carry

    lax.fori_loop(1, pairs, greet_rank, 0)
    pl.when(has_up)(lambda: greet(col, depth - 1))
    pl.when(has_down)(lambda: greet(col, depth + 1))
    one = jnp.int32(1)
    none = jnp.int32(0)
    depth_sides = jnp.where(has_up, one, none) + jnp.where(has_down, one, none)
    col_sides = jnp.where(has_left, one, none) + jnp.where(has_right, one, none)
    for step, present in ((-1, has_left), (1, has_right)):
        pl.when(present)(lambda step=step: greet(col + step, depth))
        pl.when(present & has_up)(lambda step=step: greet(col + step, depth - 1))
        pl.when(present & has_down)(lambda step=step: greet(col + step, depth + 1))

    def move(k, x0):
        ext[k + 1, pl.ds(LEFT + x0, 8)] = nat[k, pl.ds(x0, 8), :].reshape(8, SUB, LANES)

    def relayout(k):
        def body(i, carry):
            for u in range(4):
                move(k, pl.multiple_of(i * 32 + u * 8, 8))
            return carry

        lax.fori_loop(0, columns // 32, body, 0)

    groups = half // 8
    late = 2 if block == 2 * SMAX and groups == 8 else 0
    first = (groups - late) * 8

    def group_at(i, parity):
        if not late:
            return i
        skipped = lax.rem(2 - 2 * parity + 4 * (i - 6) + 8, 8)
        return jnp.where(i < 6, lax.rem(2 - 2 * parity + i + 1 + i // 3, 8), skipped)

    def encode_slice(slot, k):
        def body(i, carry):
            g = group_at(i, side)
            low = ext[k + 1, pl.ds(LEFT + g * 8, 8)]
            high = ext[k + 1, pl.ds(LEFT + half + g * 8, 8)]
            zsend[slot, pl.ds(i * 8, 8)] = pack(density_code(low), density_code(high))
            return carry

        lax.fori_loop(0, half // 8, body, 0)

    for k in (0, slices - 1):
        loads[k].wait()
        relayout(k)
    encode_slice(0, slices - 1)
    encode_slice(1, 0)
    pl.semaphore_wait(barrier, pairs - 1 + depth_sides + col_sides + col_sides * depth_sides)

    def remote(src, dst, send, recv, c, d):
        return pltpu.make_async_remote_copy(
            src_ref=src, dst_ref=dst, send_sem=send, recv_sem=recv, device_id=at(c, d), device_id_type=MESH
        )

    tail = pl.ds((3 + 2 * side) * 8 if late else half - SMAX, SMAX)
    parts = [(0, pl.ds(0, first))] + ([(1, pl.ds(first, late * 8))] if late else [])
    z_copies = [
        [
            remote(zsend.at[slot, span], zrecv.at[slot, span], z_send.at[slot, n], z_recv.at[slot, n], col, to)
            for n, span in parts
        ]
        for slot, to in ((0, depth + 1), (1, depth - 1))
    ]
    c_copies = [
        remote(zsend.at[0, tail], crecv.at[0], c_send.at[0], c_recv.at[0], col + 1, depth + 1),
        remote(zsend.at[1, tail], crecv.at[1], c_send.at[1], c_recv.at[1], col + 1, depth - 1),
    ]
    z_out = (has_down, has_up)
    z_in = (has_up, has_down)
    for slot in range(2):
        pl.when(z_out[slot])(z_copies[slot][0].start)
        pl.when(z_out[slot] & has_right)(c_copies[slot].start)
    for slot in range(2 if late else 0):
        pl.when(z_out[slot])(z_copies[slot][1].start)

    for k in range(1, slices - 1):
        loads[k].wait()
        for x0 in (0, columns - 16, columns - 8):
            move(k, x0)
    inner = pl.ds(1, slices)
    to_right = remote(ext.at[inner, pl.ds(columns, LEFT)], lrecv, col_send.at[0], col_recv.at[0], col + 1, depth)
    to_left = remote(ext.at[inner, pl.ds(LEFT, 1)], rrecv, col_send.at[1], col_recv.at[1], col - 1, depth)
    pl.when(has_right)(to_right.start)
    pl.when(has_left)(to_left.start)

    def relayout_inner(k, carry):
        def body(i, inner_carry):
            for u in range(4):
                move(k, pl.multiple_of(8 + jnp.minimum(i * 32 + u * 8, columns - 32), 8))
            return inner_carry

        return lax.fori_loop(0, columns // 32, body, carry)

    lax.fori_loop(1, slices - 1, relayout_inner, 0)

    source = lax.broadcasted_iota(jnp.int32, (LANES, LANES), 0)
    target = lax.broadcasted_iota(jnp.int32, (LANES, LANES), 1)

    def taps(distance):
        distance = jnp.abs(distance)
        return jnp.where(distance == 0, 0.5, jnp.where(distance == 1, 0.1875, jnp.where(distance == 2, 0.0625, 0.0)))

    weights[0:LANES, :] = taps(source - target).astype(jnp.bfloat16)
    shift = jnp.where(source < LANES // 2, LANES, -LANES)
    weights[LANES : 2 * LANES, :] = taps(source + shift - target).astype(jnp.bfloat16)
    for copy in small:
        copy.wait()

    shape = (group, SUB, LANES)
    lane = lax.broadcasted_iota(jnp.int32, (SUB, LANES), 1)
    sub = lax.broadcasted_iota(jnp.int32, (SUB, LANES), 0)
    not_first = jnp.where(sub == 0, 0.0, 1.0)[None]
    not_last = jnp.where(sub == SUB - 1, 0.0, 1.0)[None]
    edge_mask = jnp.where(lane < LANES // 2, not_last[0], not_first[0])[None]

    def pick(mask, first, second):
        return jnp.where(jnp.broadcast_to(mask[None], first.shape), first, second)

    def shade(k, x0, lhs):
        for g in range(block // group):
            row = LEFT + x0 + g * group - offsets[k]
            rows = group * SUB
            window = [ext[k + 1, row + i] for i in range(-1, group + 1)]
            center = jnp.stack(window[1:-1])
            dx = jnp.stack(window[2:]) - jnp.stack(window[:-2])
            dz = jnp.stack([ext[k + 2, row + i] - ext[k, row + i] for i in range(group)])
            before = pick(lane == LANES - 1, pltpu.roll(center, 1, 1) * not_first, center)
            after = pick(lane == 0, pltpu.roll(center, SUB - 1, 1) * not_last, center)
            dy = pltpu.roll(after, LANES - 1, 2) - pltpu.roll(before, 1, 2)
            square = dx * dx + dy * dy + dz * dz
            lambert = (0.48 * dx + 0.6 * dy + 0.64 * dz) * lax.rsqrt(jnp.maximum(square, 4.0))
            center_sq = center * center
            opacity = 1.0 - jnp.exp(-absorb * center_sq * center_sq)
            halved = opacity * (0.1 + 0.4 * jnp.abs(lambert))
            tilt = halved * jnp.tanh(center)
            green = halved + halved * jnp.tanh(0.5 - 0.5 * center_sq)
            for ch, value in enumerate((halved + tilt, green, halved - tilt, opacity)):
                edge = pick(lane < LANES // 2, pltpu.roll(value, SUB - 1, 1), pltpu.roll(value, 1, 1)) * edge_mask
                place = pl.ds((ch * block + g * group) * SUB, rows)
                lhs[place, 0:LANES] = value.reshape(rows, LANES).astype(jnp.bfloat16)
                lhs[place, LANES : 2 * LANES] = edge.reshape(rows, LANES).astype(jnp.bfloat16)

    def resample(k, x0, lhs):
        value = jnp.dot(lhs[...], weights[...], preferred_element_type=jnp.float32)
        res[k, :, pl.ds(x0, block)] = value.reshape(4, block, SUB, LANES)

    def run(count, place):
        shade(*place(0), lhs0)

        def pair(i, last):
            resample(*place(2 * i), lhs0)
            shade(*place(2 * i + 1), lhs1)
            resample(*place(2 * i + 1), lhs1)
            if not last:
                shade(*place(2 * i + 2), lhs0)

        def body(i, carry):
            pair(i, False)
            return carry

        lax.fori_loop(0, count // 2 - 1, body, 0)
        pair(count // 2 - 1, True)

    left_blocks = -(-LEFT // block)
    assert left_blocks % 2 == 1
    mid_count = pairs - left_blocks // 2 - 1
    rim_count = pairs - mid_count
    mid_start = left_blocks // 2 + side
    mid_slices = slices - 2
    early = 2

    def give_place(t, first, count):
        t = jnp.int32(t)
        slot = lax.rem(first + lax.rem(t, count), pairs)
        return 1 + t // count, (2 * slot + 1 - side) * block

    def keep_place(t, first):
        t = jnp.int32(t)
        return first + t // pairs, (2 * lax.rem(t, pairs) + side) * block

    run(mid_slices * mid_count, lambda t: give_place(t, mid_start, mid_count))

    pl.when(has_right)(to_right.wait_send)
    pl.when(has_left)(to_left.wait_send)

    @pl.when(has_left)
    def _():
        to_right.wait_recv()
        ext[1 : slices + 1, 0:LEFT] = lrecv[...]

    @pl.when(has_right)
    def _():
        to_left.wait_recv()
        ext[1 : slices + 1, LEFT + columns : LEFT + columns + 1] = rrecv[...]

    @pl.when(jnp.logical_not(has_left))
    def _():
        ext[:, 0:LEFT] = jnp.zeros((slices + 2, LEFT, SUB, LANES), jnp.float32)

    @pl.when(jnp.logical_not(has_right))
    def _():
        ext[:, LEFT + columns : LEFT + columns + 1] = jnp.zeros((slices + 2, 1, SUB, LANES), jnp.float32)

    run(mid_slices * rim_count, lambda t: give_place(t, mid_start + mid_count, rim_count))
    run(early * pairs, lambda t: keep_place(t, 1))

    def decode_slice(slot, plane, start, stop):
        def body(i, carry):
            g = group_at(i, 1 - side)
            word = zrecv[slot, pl.ds(i * 8, 8)]
            ext[plane, pl.ds(LEFT + g * 8, 8)] = density_value(low_half(word))
            ext[plane, pl.ds(LEFT + half + g * 8, 8)] = density_value(high_half(word))
            return carry

        lax.fori_loop(start, stop, body, 0)

    for slot, plane in ((0, 0), (1, slices + 1)):
        @pl.when(z_in[slot])
        def _(slot=slot, plane=plane):
            z_copies[slot][0].wait_recv()
            decode_slice(slot, plane, 0, groups - late)

        @pl.when(z_in[slot] & has_left)
        def _(slot=slot, plane=plane):
            c_copies[slot].wait_recv()
            ext[plane, pl.ds(1, SMAX)] = density_value(high_half(crecv[slot]))

        @pl.when(jnp.logical_not(z_in[slot]))
        def _(plane=plane):
            ext[plane] = jnp.zeros(ext.shape[1:], jnp.float32)

    def finish_block(number):
        start = number * block
        shade(0, start, lhs0)
        resample(0, start, lhs0)
        shade(slices - 1, start, lhs1)
        resample(slices - 1, start, lhs1)

    def column_partial(x):
        flip = [flips[x + u] for u in range(lump)]
        colour = [None] * 3
        transmit = None
        for i in range(slices):
            depths = [i + flip[u] * (slices - 1 - 2 * i) for u in range(lump)]
            through = 1.0 - jnp.stack([res[depths[u], 3, x + u] for u in range(lump)])
            for ch in range(3):
                value = jnp.stack([res[depths[u], ch, x + u] for u in range(lump)])
                colour[ch] = value if i == 0 else colour[ch] + transmit * value
            transmit = through if i == 0 else transmit * through
        return colour, transmit

    def store_codes(ref, slot, x, colour, opacity):
        span = pl.ds(x, lump)
        ref[slot, 0, span] = pack(image_code(colour[0]), image_code(colour[1]))
        ref[slot, 1, span] = pack(image_code(colour[2]), image_code(opacity))

    def load_codes(first, second):
        colour = [image_value(low_half(first)), image_value(high_half(first)), image_value(low_half(second))]
        return colour, image_value(high_half(second))

    def y_copy(slot):
        return remote(ysend.at[slot], yrecv.at[slot], y_send.at[slot], y_recv.at[slot], col, depth + 1 - 2 * side)

    def i_copy(slot):
        return remote(isend.at[slot], irecv.at[rank], i_send.at[slot], i_recv.at[rank], col, 2 * slot + side)

    def give(i, carry):
        slot = lax.rem(rank + 1 + i, pairs)
        number = 2 * slot + 1 - side
        finish_block(number)

        for x in range(0, block, lump):
            colour, transmit = column_partial(number * block + x)
            store_codes(ysend, slot, x, colour, 1.0 - transmit)
        y_copy(slot).start()
        return carry

    lax.fori_loop(0, pairs, give, 0)
    for slot, plane in ((0, 0), (1, slices + 1)) if late else ():
        @pl.when(z_in[slot])
        def _(slot=slot, plane=plane):
            z_copies[slot][1].wait_recv()
            decode_slice(slot, plane, groups - late, groups)

    run((mid_slices - early) * pairs, lambda t: keep_place(t, 1 + early))

    def keep(i, carry):
        slot = lax.rem(rank + 1 + i, pairs)
        number = 2 * slot + side
        finish_block(number)

        for x in range(0, block, lump):
            colour, transmit = column_partial(number * block + x)
            for ch in range(3):
                kept[ch, pl.ds(x, lump)] = colour[ch]
            kept[3, pl.ds(x, lump)] = transmit
        y_copy(slot).wait_recv()

        for x in range(0, block, lump):
            span = pl.ds(x, lump)
            theirs, their_opacity = load_codes(yrecv[slot, 0, span], yrecv[slot, 1, span])
            their_transmit = 1.0 - their_opacity
            mine = [kept[ch, span] for ch in range(3)]
            my_transmit = kept[3, span]
            flip = [jnp.full((SUB, LANES), flips[number * block + x + u], jnp.int32) for u in range(lump)]
            mine_first = jnp.stack(flip) == side
            front_transmit = jnp.where(mine_first, my_transmit, their_transmit)
            colour = []
            for ch in range(3):
                front = jnp.where(mine_first, mine[ch], theirs[ch])
                behind = jnp.where(mine_first, theirs[ch], mine[ch])
                colour.append(front + front_transmit * behind)
            opacity = 1.0 - my_transmit * their_transmit

            store_codes(isend, slot, x, colour, opacity)
            store_codes(irecv, rank, x, colour, opacity)
        pl.when(i < pairs - 1)(lambda: i_copy(slot).start())
        return carry

    lax.fori_loop(0, pairs, keep, 0)

    def arrive(i, carry):
        slot = lax.rem(rank + i, pairs)
        remote(
            isend.at[slot], irecv.at[slot], i_send.at[slot], i_recv.at[slot], col, 2 * slot + side
        ).wait_recv()
        return carry

    lax.fori_loop(1, pairs, arrive, 0)

    for x in range(0, block, lump):
        flip = [flips[depth * block + x + u] for u in range(lump)]
        colour = [None] * 3
        transmit = None
        for i in range(pairs):
            slot = [i + flip[u] * (pairs - 1 - 2 * i) for u in range(lump)]
            words = [jnp.stack([irecv[slot[u], part, x + u] for u in range(lump)]) for part in range(2)]
            value, opacity = load_codes(*words)
            for ch in range(3):
                colour[ch] = value[ch] if i == 0 else colour[ch] + transmit * value[ch]
            transmit = 1.0 - opacity if i == 0 else transmit * (1.0 - opacity)
        for ch in range(3):
            final[ch, pl.ds(x, lump)] = colour[ch]
        final[3, pl.ds(x, lump)] = 1.0 - transmit
    part = min(8, block)
    for ch in range(4):
        for x0 in range(0, block, part):
            out[ch, x0 : x0 + part, :] = final[ch, x0 : x0 + part].reshape(part, height)

    for slot in range(2):
        for copy in z_copies[slot]:
            pl.when(z_out[slot])(copy.wait_send)
        pl.when(z_out[slot] & has_right)(c_copies[slot].wait_send)

    def left_y(i, carry):
        y_copy(i).wait_send()
        return carry

    lax.fori_loop(0, pairs, left_y, 0)

    def left_i(i, carry):
        i_copy(lax.rem(rank + i, pairs)).wait_send()
        return carry

    lax.fori_loop(1, pairs, left_i, 0)


def on_device(density, offsets, view_flip):
    col_count, depth_count = lax.axis_size("col"), lax.axis_size("depth")
    slices, columns, height = density.shape
    block = columns // depth_count
    pairs = depth_count // 2
    half = columns // 2
    f32, i32 = jnp.float32, jnp.int32
    dma = pltpu.SemaphoreType.DMA
    image = pltpu.VMEM((pairs, 2, block, SUB, LANES), i32)
    scratch = [
        pltpu.SMEM((slices,), i32),
        pltpu.SMEM((columns,), i32),
        pltpu.VMEM((2 * LANES, LANES), jnp.bfloat16),
        pltpu.VMEM((slices, columns, height), f32),
        pltpu.VMEM((slices + 2, LEFT + columns + 1, SUB, LANES), f32),
        pltpu.VMEM((slices, LEFT, SUB, LANES), f32),
        pltpu.VMEM((slices, 1, SUB, LANES), f32),
        pltpu.VMEM((2, half, SUB, LANES), i32),
        pltpu.VMEM((2, half, SUB, LANES), i32),
        pltpu.VMEM((2, SMAX, SUB, LANES), i32),
        pltpu.VMEM((4 * block * SUB, 2 * LANES), jnp.bfloat16),
        pltpu.VMEM((4 * block * SUB, 2 * LANES), jnp.bfloat16),
        pltpu.VMEM((slices, 4, columns, SUB, LANES), f32),
        pltpu.VMEM((4, block, SUB, LANES), f32),
        image, image, image, image,
        pltpu.VMEM((4, block, SUB, LANES), f32),
        dma((2,)),
        dma((slices,)),
        dma((2,)), dma((2,)), dma((2, 2)), dma((2, 2)), dma((2,)), dma((2,)),
        dma((pairs,)), dma((pairs,)), dma((pairs,)), dma((pairs,)),
    ]
    vmem = pl.BlockSpec(memory_space=pltpu.VMEM)
    hbm = pl.BlockSpec(memory_space=pltpu.HBM)
    return pl.pallas_call(
        functools.partial(kernel, col_count, depth_count),
        out_shape=jax.ShapeDtypeStruct((4, block, height), f32),
        in_specs=[hbm, hbm, hbm],
        out_specs=vmem,
        scratch_shapes=scratch,
        compiler_params=pltpu.CompilerParams(
            collective_id=0, has_side_effects=True, vmem_limit_bytes=48 * 2**20
        ),
    )(density, offsets, view_flip)


def solution(mesh):
    in_specs = (P("depth", "col", None), P("depth"), P("col"))
    out_specs = P(None, ("col", "depth"), None)
    return jax.shard_map(
        on_device, mesh=mesh, in_specs=in_specs, out_specs=out_specs, check_vma=False
    )
```
